128 devices in a mesh: tm: 4 (over x_lo, core), cell: 32 (over z, y, x_hi).
Axes of the slice: x: 4 (x_hi: 2, x_lo: 2; x = x_hi * 2 + x_lo), y: 4, z: 4, core: 2. Of those that a mesh axis runs over, the one named last changes fastest.
Arguments:
- coords: float32 [4, 64, 16384], P('tm', None, 'cell'), may hold values from -8 to 8
- potentials: float32 [4, 16384], P('tm', 'cell'), may hold values from -6 to 202
Outputs:
- beliefs: float32 [4, 16384], P('tm', 'cell')
The draws below stay inside these ranges and needn't reach their ends.
All inputs are finite; a program needn't handle non-finite values.
Results may differ from the reference program's by a relative error of at most 0.00011.
Values sent between devices are 32-bit elements; how exact they have to be, the bound alone decides.
No kernel may reach another device: no remote copies, remote signals or barrier semaphores. Data moves between devices by JAX's collectives and lax.ppermute only.
A program may use at most 64 MiB of HBM per device.

```python
import math
import jax
import jax.numpy as jnp
from jax import lax

DIM = 64
TIMES = 4
CELLS = 16384


def draw_coords(key, part):
    base = jax.random.normal(jax.random.fold_in(key, 71), (TIMES, DIM, CELLS), jnp.float32)
    return jnp.clip(base * 0.25, -8.0, 8.0)


def draw_potentials(key, part):
    own_key = jax.random.fold_in(key, 72)
    return jnp.clip(jax.random.normal(own_key, (TIMES, CELLS), jnp.float32), -6.0, 6.0)


def setup_inputs(seed: int = 0) -> dict:
    arg_keys = jax.random.split(jax.random.key(seed), 3)
    coords = draw_coords(jax.random.fold_in(arg_keys[2], 71), 0)
    potentials = draw_potentials(jax.random.fold_in(arg_keys[2], 71), 0)
    return dict(coords=coords, potentials=potentials)


EPS = 1.0


def message(sources, belief, targets):
    src_sq = jnp.sum(sources * sources, axis=0)
    width = min(512, targets.shape[1])
    blocks = targets.reshape(targets.shape[0], targets.shape[1] // width, width).transpose(1, 0, 2)

    def one_block(block):
        cross = lax.dot_general(sources, block, (((0,), (0,)), ((), ())), precision=lax.Precision.HIGHEST, preferred_element_type=jnp.float32)
        dist = (src_sq[:, None] + jnp.sum(block * block, axis=0)[None, :]) - 2.0 * cross
        score = belief[:, None] - dist / EPS
        return jax.nn.logsumexp(score, axis=0)

    return lax.map(one_block, blocks).reshape(-1)


def reference(coords, potentials):
    offset = math.log(CELLS)
    rows = [potentials[0]]
    for step in range(TIMES - 1):
        result = message(coords[step], rows[-1], coords[step + 1])
        rows.append(result - offset + potentials[step + 1])
    return jnp.stack(rows, axis=0)
```

```python
import functools
import math

import jax
import jax.numpy as jnp
from jax import lax
from jax.experimental import pallas as pl
from jax.experimental.pallas import tpu as pltpu
from jax.sharding import PartitionSpec as P

LOG2E = math.log2(math.e)
LN2 = math.log(2.0)
LANES = 128
DEPTH = 256
VMEM_LIMIT = 50 * 2**20

F32 = jnp.float32
BF16 = jnp.bfloat16


def params():
    return pltpu.CompilerParams(vmem_limit_bytes=VMEM_LIMIT)


def halves(x):
    high = x.astype(BF16)
    return high, (x - high.astype(F32)).astype(BF16)


def bias_rows(first, w, n):
    w1 = w.astype(BF16).astype(F32)
    w2 = (w - w1).astype(BF16).astype(F32)
    w3 = w - w1 - w2
    row = lax.broadcasted_iota(jnp.int32, (16, n), 0)
    other = 3 - first
    block = jnp.where(row == first, w1, jnp.where(row == first + 1, w2, jnp.where(row == first + 2, w3, 0.0)))
    block = jnp.where((row >= other) & (row < other + 3), 1.0, block)
    return jnp.concatenate([block.astype(BF16), jnp.zeros((48, n), BF16)], axis=0)


def row_side(x, w):
    high, low = halves(x * (2.0 * LOG2E))
    return jnp.concatenate([high, high, low, bias_rows(3, w, x.shape[1])], axis=0)


def col_side(x, w):
    high, low = halves(x)
    return jnp.concatenate([high, low, high, bias_rows(0, w, x.shape[1])], axis=0)


def square(x):
    return jnp.sum(x * x, axis=0, keepdims=True)


def lse2(parts):
    top = functools.reduce(jnp.maximum, parts)
    return top + jnp.log2(functools.reduce(jnp.add, [jnp.exp2(p - top) for p in parts]))


def times(a, b):
    return lax.dot_general(a, b, (((1,), (0,)), ((), ())), preferred_element_type=F32)


def over_columns(rows_t, col_chunk, chunks, width, scores, top):
    n = scores.shape[0]
    for k in range(chunks):
        s = times(rows_t, col_chunk(k))
        scores[:, k * width : (k + 1) * width] = s
        best = functools.reduce(jnp.maximum, [s[:, i : i + LANES] for i in range(0, width, LANES)])
        top[...] = best if k == 0 else jnp.maximum(top[...], best)
    step = 64
    for r in range(0, n, step):
        m = jnp.max(top[r : r + step, :], axis=1, keepdims=True)
        acc = jnp.zeros((step, LANES), F32)
        for i in range(0, chunks * width, LANES):
            acc = acc + jnp.exp2(scores[r : r + step, i : i + LANES] - m)
        total = jnp.sum(acc, axis=1, keepdims=True)
        top[r : r + step, :] = jnp.broadcast_to(m + jnp.log2(total), (step, LANES))
    return jnp.transpose(top[...])[0:1, :]


def pack_kernel(place, coords, pot, full, *slices):
    here = place[0]
    dims, n = coords.shape[1:]
    full[0:dims, :] = coords[0]
    full[dims : dims + 8, :] = jnp.broadcast_to(pot[...], (8, n))
    for k, out in enumerate(slices):
        at = pl.multiple_of(lax.rem(here + k, len(slices)) * LANES, LANES)
        out[...] = full[:, pl.ds(at, LANES)]


def spread_kernel(place, own, *rest, root):
    *came, out = rest
    turn = lax.rem(place[0] + len(came) + 1 - root, len(came) + 1)
    x = own[...]
    for k, c in enumerate(came):
        x = jnp.where(turn == k + 1, c[...], x)
    out[...] = jnp.broadcast_to(x[None], out.shape)


def first_kernel(rows, cols, out, scores, top):
    dims = rows.shape[0] - 8
    y = rows[0:dims, :]
    rows_t = jnp.transpose(row_side(y, jnp.zeros((1, y.shape[1]), F32)))

    def chunk(k):
        parts = []
        for i in range(4 * k, 4 * k + 4):
            x = cols[i, 0:dims, :]
            parts.append(col_side(x, (cols[i, dims : dims + 1, :] - square(x)) * LOG2E))
        return jnp.concatenate(parts, axis=1)

    out[...] = over_columns(rows_t, chunk, cols.shape[0] // 4, 4 * LANES, scores, top)


def second_kernel(offset, rows, cols, own, *rest):
    *came, belief, out = rest
    dims = rows.shape[0] - 8
    y = rows[0:dims, :]
    y2 = square(y)
    b = lse2([own[...]] + [c[...] for c in came]) * LN2 - y2 - offset + rows[dims : dims + 1, :]
    belief[...] = b
    rows_t = jnp.transpose(row_side(y, (b - y2) * LOG2E))
    lines = []
    for k in range(0, cols.shape[0], 2):
        parts = []
        for i in (k, k + 1):
            parts.append(col_side(cols[i, 0:dims, :], jnp.zeros((1, LANES), F32)))
        s = times(rows_t, jnp.concatenate(parts, axis=1))
        m = jnp.max(s, axis=0, keepdims=True)
        line = m + jnp.log2(jnp.sum(jnp.exp2(s - m), axis=0, keepdims=True))
        lines += [line[:, 0:LANES], line[:, LANES:]]
    out[...] = jnp.broadcast_to(jnp.concatenate(lines, axis=0)[None], out.shape)


def third_kernel(offset, place, rows, cols, came, out, scores, top, belief):
    dims = rows.shape[0] - 8
    n = cols.shape[0]
    best = came[0]
    for i in range(1, n):
        best = jnp.maximum(best, came[i])
    total = jnp.exp2(came[0] - best)
    for i in range(1, n):
        total = total + jnp.exp2(came[i] - best)
    belief[...] = (best + jnp.log2(total)) * LN2
    rows_t = jnp.transpose(row_side(rows[0:dims, :], jnp.zeros((1, rows.shape[1]), F32)))

    def chunk(k):
        parts = []
        for i in range(4 * k, 4 * k + 4):
            x = cols[i, 0:dims, :]
            x2 = square(x)
            b = belief[i : i + 1, :] - x2 - offset + cols[i, dims : dims + 1, :]
            belief[i : i + 1, :] = b
            parts.append(col_side(x, (b - x2) * LOG2E))
        return jnp.concatenate(parts, axis=1)

    wide = rows.shape[1]
    out[:, 0:wide] = over_columns(rows_t, chunk, n // 4, 4 * LANES, scores, top)
    out[:, wide:] = belief[pl.ds(place[1], 1), :]


def last_kernel(offset, place, pot, belief, rows, own, *rest):
    *came, out = rest
    here = place[0]
    dims = rows.shape[0] - 8
    wide = rows.shape[1]
    times_ = len(came) + 1
    got = [own] + list(came)
    end = lse2([g[:, 0:wide] for g in got]) * LN2 - square(rows[0:dims, :]) - offset + rows[dims : dims + 1, :]
    pieces = [got[(2 - source) % times_][:, wide:] for source in range(times_)]
    middle = jnp.concatenate(pieces, axis=1)
    out[...] = jnp.where(here == 0, pot[...], jnp.where(here == 1, belief[...], jnp.where(here == 2, middle, end)))


def body(coords, potentials):
    _, dims, n = coords.shape
    groups = lax.axis_size("tm")
    cells = lax.axis_size("cell")
    offset = math.log(n * cells)
    tall = dims + 8
    wide = cells * n // groups
    here = lax.axis_index("tm")
    place = jnp.stack([here, lax.axis_index("cell")]).astype(jnp.int32)
    smem = pl.BlockSpec(memory_space=pltpu.SMEM)
    vmem = pl.BlockSpec(memory_space=pltpu.VMEM)

    def arr(*shape):
        return jax.ShapeDtypeStruct(shape, F32)

    def turned(x, k):
        return lax.ppermute(x, "tm", [(i, (i + k) % groups) for i in range(groups)])

    full, *slices = pl.pallas_call(
        pack_kernel,
        out_shape=[arr(tall, n)] + [arr(tall, LANES)] * groups,
        in_specs=[smem, vmem, vmem],
        compiler_params=params(),
        name="pack",
    )(place, coords, potentials)
    came = [turned(slices[k], k) for k in range(1, groups)]

    def spread(root):
        return pl.pallas_call(
            functools.partial(spread_kernel, root=root),
            out_shape=arr(cells, tall, LANES),
            in_specs=[smem] + [vmem] * groups,
            compiler_params=params(),
            name="spread",
        )(place, slices[0], *came)

    def whole(x):
        return lax.all_to_all(x, "cell", 0, 0, tiled=True)

    cols0 = whole(spread(0))
    whole_shards = [full] + [turned(full, k) for k in range(1, groups)]

    def shard(root):
        pick = lax.rem(here + groups - root, groups)
        x = whole_shards[0]
        for k in range(1, groups):
            x = jnp.where(pick == k, whole_shards[k], x)
        return x

    rows1 = shard(1)
    rows3 = shard(3)
    cols2 = whole(spread(2))

    scratch = [pltpu.VMEM((n, wide), F32), pltpu.VMEM((n, LANES), F32)]
    part = pl.pallas_call(
        first_kernel, out_shape=arr(1, n), scratch_shapes=scratch, compiler_params=params(), name="first"
    )(rows1, cols0)
    parts = [turned(part, k) for k in range(1, groups)]
    belief1, mine = pl.pallas_call(
        functools.partial(second_kernel, offset),
        out_shape=[arr(1, n), arr(cells, cells, LANES)],
        compiler_params=params(),
        name="second",
    )(rows1, cols2, part, *parts)
    seen = whole(mine)
    part = pl.pallas_call(
        functools.partial(third_kernel, offset),
        out_shape=arr(1, n + LANES),
        in_specs=[smem, vmem, vmem, vmem],
        scratch_shapes=scratch + [pltpu.VMEM((cells, LANES), F32)],
        compiler_params=params(),
        name="third",
    )(place, rows3, cols2, seen)
    parts = [turned(part, k) for k in range(1, groups)]
    return pl.pallas_call(
        functools.partial(last_kernel, offset),
        out_shape=arr(1, n),
        in_specs=[smem] + [vmem] * (3 + groups),
        compiler_params=params(),
        name="last",
    )(place, potentials, belief1, rows3, part, *parts)


def solution(mesh):
    return jax.shard_map(
        body,
        mesh=mesh,
        in_specs=(P("tm", None, "cell"), P("tm", "cell")),
        out_specs=P("tm", "cell"),
        check_vma=False,
    )
```

```python
import functools
import math

import jax
import jax.numpy as jnp
from jax import lax
from jax.experimental import pallas as pl
from jax.experimental.pallas import tpu as pltpu
from jax.sharding import PartitionSpec as P

LOG2E = math.log2(math.e)
LN2 = math.log(2.0)
LANES = 128
VMEM_LIMIT = 50 * 2**20

F32 = jnp.float32
BF16 = jnp.bfloat16

GROUPS = 4
PLACES = 16
SIDES = 2


def params():
    return pltpu.CompilerParams(vmem_limit_bytes=VMEM_LIMIT)


def halves(x):
    high = x.astype(BF16)
    return high, (x - high.astype(F32)).astype(BF16)


def bias_rows(first, w, n):
    w1 = w.astype(BF16).astype(F32)
    w2 = (w - w1).astype(BF16).astype(F32)
    w3 = w - w1 - w2
    row = lax.broadcasted_iota(jnp.int32, (16, n), 0)
    other = 3 - first
    block = jnp.where(row == first, w1, jnp.where(row == first + 1, w2, jnp.where(row == first + 2, w3, 0.0)))
    block = jnp.where((row >= other) & (row < other + 3), 1.0, block)
    return jnp.concatenate([block.astype(BF16), jnp.zeros((48, n), BF16)], axis=0)


def row_side(x, w):
    high, low = halves(x * (2.0 * LOG2E))
    return jnp.concatenate([high, high, low, bias_rows(3, w, x.shape[1])], axis=0)


def col_side(x, w):
    high, low = halves(x)
    return jnp.concatenate([high, low, high, bias_rows(0, w, x.shape[1])], axis=0)


def square(x):
    return jnp.sum(x * x, axis=0, keepdims=True)


def largest(parts):
    return functools.reduce(jnp.maximum, parts)


def added(parts):
    while len(parts) > 1:
        parts = [functools.reduce(jnp.add, parts[i : i + 2]) for i in range(0, len(parts), 2)]
    return parts[0]


def lse2(parts):
    top = largest(parts)
    return top + jnp.log2(added([jnp.exp2(p - top) for p in parts]))


def times(a, b):
    return lax.dot_general(a, b, (((1,), (0,)), ((), ())), preferred_element_type=F32)


def piped(count, start, finish):
    start(0)
    for k in range(count):
        if k + 1 < count:
            start(k + 1)
        finish(k)


def more(state, parts):
    best = largest(parts)
    if state is None:
        return best, added([jnp.exp2(p - best) for p in parts])
    top, total = state
    new = jnp.maximum(top, best)
    return new, total * jnp.exp2(top - new) + added([jnp.exp2(p - new) for p in parts])


def over_columns(rows_t, col_chunk, chunks, width, bufs, top, total):
    n = rows_t.shape[0]
    step = 32

    def start(k):
        bufs[k % 2][...] = times(rows_t, col_chunk(k))

    def finish(k):
        buf = bufs[k % 2]
        for r in range(0, n, step):
            at = slice(r, r + step)
            state = None if k == 0 else (top[at, :], total[at, :])
            a, b = more(state, [buf[at, i : i + LANES] for i in range(0, width, LANES)])
            top[at, :] = a
            total[at, :] = b

    piped(chunks, start, finish)
    a = jnp.transpose(top[...])
    b = jnp.transpose(total[...])
    best = jnp.max(a, axis=0, keepdims=True)
    return best + jnp.log2(jnp.sum(b * jnp.exp2(a - best), axis=0, keepdims=True))


def over_rows(rows_t, col_chunk, chunks, width, bufs):
    n = rows_t.shape[0]
    step = 8
    lines = []

    def start(k):
        bufs[k % 2][:, 0:width] = times(rows_t, col_chunk(k))

    def finish(k):
        buf = bufs[k % 2]
        for i in range(0, width, LANES):
            state = None
            for r in range(0, n, 32 * step):
                state = more(state, [buf[q : q + step, i : i + LANES] for q in range(r, r + 32 * step, step)])
            a, b = state
            best = jnp.max(a, axis=0, keepdims=True)
            lines.append(best + jnp.log2(jnp.sum(b * jnp.exp2(a - best), axis=0, keepdims=True)))

    piped(chunks, start, finish)
    return lines


def spread_kernel(place, own, own_pot, other, other_pot, out, target):
    core = place[1]
    _, dims, n = own.shape
    half = n // 2
    at = pl.multiple_of(core * half, half)
    x = jnp.where(core == 0, own[0, :, pl.ds(at, half)], other[0, :, pl.ds(at, half)])
    p = jnp.where(core == 0, own_pot[:, pl.ds(at, half)], other_pot[:, pl.ds(at, half)])
    for i in range(out.shape[0]):
        out[i, 0:dims, :] = x
        out[i, dims:, :] = jnp.broadcast_to(p, (8, half))
    target[0:dims, :] = jnp.where(core == 0, other[0], own[0])
    target[dims:, :] = jnp.broadcast_to(jnp.where(core == 0, other_pot[...], own_pot[...]), (8, n))


def order_kernel(place, own, other, out):
    n = own.shape[1]
    first = place[2] == 0
    out[:, 0:n] = jnp.where(first, own[...], other[...])
    out[:, n:] = jnp.where(first, other[...], own[...])


def first_kernel(place, rows, cols, out, one, two, top, total):
    dims = rows.shape[0] - 8

    @pl.when(place[0] == 0)
    def _():
        y = rows[0:dims, :]
        rows_t = jnp.transpose(row_side(y, jnp.zeros((1, y.shape[1]), F32)))

        def chunk(k):
            parts = []
            for i in range(4 * k, 4 * k + 4):
                x = cols[i, 0:dims, :]
                parts.append(col_side(x, (cols[i, dims : dims + 1, :] - square(x)) * LOG2E))
            return jnp.concatenate(parts, axis=1)

        out[...] = over_columns(rows_t, chunk, cols.shape[0] // 4, 4 * cols.shape[2], (one, two), top, total)

    @pl.when(place[0] != 0)
    def _():
        out[...] = jnp.zeros(out.shape, F32)


def second_kernel(offset, place, rows, cols, *rest):
    *came, belief, out, one, two = rest
    dims = rows.shape[0] - 8

    @pl.when(place[0] == 0)
    def _():
        belief[...] = jnp.zeros(belief.shape, F32)
        out[...] = jnp.zeros(out.shape, F32)

    @pl.when(place[0] != 0)
    def _():
        y = rows[0:dims, :]
        y2 = square(y)
        b = lse2([c[...] for c in came]) * LN2 - y2 - offset + rows[dims : dims + 1, :]
        n = b.shape[1] // 2
        belief[...] = jnp.where(place[2] == 0, b[:, 0:n], b[:, n:])
        rows_t = jnp.transpose(row_side(y, (b - y2) * LOG2E))

        def chunk(k):
            parts = []
            for i in (2 * k, 2 * k + 1):
                parts.append(col_side(cols[i, 0:dims, :], jnp.zeros((1, cols.shape[2]), F32)))
            return jnp.concatenate(parts, axis=1)

        lines = over_rows(rows_t, chunk, cols.shape[0] // 2, 2 * cols.shape[2], (one, two))
        out[...] = jnp.broadcast_to(jnp.concatenate(lines, axis=0)[None], out.shape)


def third_kernel(offset, place, rows, cols, came, out, one, two, top, total, belief):
    dims = rows.shape[0] - 8
    n = cols.shape[0]
    wide = rows.shape[1]

    @pl.when(place[0] == 0)
    def _():
        out[...] = jnp.zeros(out.shape, F32)

    @pl.when(place[0] != 0)
    def _():
        belief[...] = lse2([came[i] for i in range(n)]) * LN2
        rows_t = jnp.transpose(row_side(rows[0:dims, :], jnp.zeros((1, wide), F32)))

        def chunk(k):
            parts = []
            for i in range(4 * k, 4 * k + 4):
                x = cols[i, 0:dims, :]
                x2 = square(x)
                b = jnp.concatenate([belief[2 * i : 2 * i + 1, :], belief[2 * i + 1 : 2 * i + 2, :]], axis=1)
                b = b - x2 - offset + cols[i, dims : dims + 1, :]
                belief[2 * i : 2 * i + 1, :] = b[:, 0:LANES]
                belief[2 * i + 1 : 2 * i + 2, :] = b[:, LANES:]
                parts.append(col_side(x, (b - x2) * LOG2E))
            return jnp.concatenate(parts, axis=1)

        out[:, 0:wide] = over_columns(rows_t, chunk, n // 4, 4 * cols.shape[2], (one, two), top, total)
        own = 2 * place[3]
        out[:, wide : wide + LANES] = belief[pl.ds(own, 1), :]
        out[:, wide + LANES :] = belief[pl.ds(own + 1, 1), :]


def last_kernel(offset, place, pot, belief, rows, own, partner, *rest):
    *came, out = rest
    here = 2 * place[0] + place[1]
    dims = rows.shape[0] - 8
    n = pot.shape[1]
    wide = rows.shape[1]
    x = rows[0:dims, :]
    line = lse2([g[:, 0:wide] for g in (own, partner, *came)]) * LN2 - square(x) - offset + rows[dims : dims + 1, :]
    end = jnp.where(place[2] == 0, line[:, 0:n], line[:, n:])
    middle = jnp.concatenate([own[:, wide:], partner[:, wide:]], axis=1)
    out[...] = jnp.where(here == 0, pot[...], jnp.where(here == 1, belief[...], jnp.where(here == 2, middle, end)))


def device(v):
    low, core, where, high = v
    return (low * 2 + core) * (PLACES * SIDES) + where * SIDES + high


def moves(low=0, core=0, high=0, of=(0, 1)):
    return [
        (device((a, b, c, d)), device((a ^ low, b ^ core, c, d ^ high)))
        for a in of
        for b in (0, 1)
        for c in range(PLACES)
        for d in (0, 1)
    ]


def body(coords, potentials):
    _, dims, n = coords.shape
    cells = lax.axis_size("cell")
    offset = math.log(n * cells)
    tall = dims + 8
    half = n // 2
    here = lax.axis_index("tm")
    spot = lax.axis_index("cell")
    place = jnp.stack([here // 2, here % 2, spot % SIDES, spot // SIDES]).astype(jnp.int32)
    smem = pl.BlockSpec(memory_space=pltpu.SMEM)
    vmem = pl.BlockSpec(memory_space=pltpu.VMEM)
    lines = PLACES * half // LANES

    def arr(*shape):
        return jax.ShapeDtypeStruct(shape, F32)

    def sent(x, **where):
        return lax.ppermute(x, ("tm", "cell"), moves(**where))

    def around(x):
        same = [[p * SIDES + d for p in range(PLACES)] for d in range(SIDES)]
        return lax.all_to_all(x, "cell", 0, 0, axis_index_groups=same, tiled=True)

    def call(kernel, name, out, ins, scratch=()):
        return pl.pallas_call(
            kernel,
            out_shape=out,
            in_specs=[smem] + [vmem] * (ins - 1),
            scratch_shapes=list(scratch),
            compiler_params=params(),
            name=name,
        )

    other = sent(coords, core=1)
    other_pot = sent(potentials, core=1)
    copies, target = call(spread_kernel, "spread", [arr(PLACES, tall, half), arr(tall, n)], 5)(
        place, coords, potentials, other, other_pot
    )
    cols = around(copies)
    rows = call(order_kernel, "order", arr(tall, 2 * n), 3)(place, target, sent(target, high=1))
    rows1 = sent(rows, low=1, of=(0,))

    bufs = [pltpu.VMEM((2 * n, 4 * half), F32)] * 2
    pair = [pltpu.VMEM((2 * n, LANES), F32)] * 2
    part = call(first_kernel, "first", arr(1, 2 * n), 3, bufs + pair)(place, rows, cols)
    parts = [sent(part, low=1, core=j, high=k, of=(0,)) for j in (0, 1) for k in (0, 1)]
    belief1, mine = call(
        functools.partial(second_kernel, offset), "second", [arr(1, n), arr(PLACES, lines, LANES)], 7, bufs
    )(place, rows1, cols, *parts)
    seen = around(mine)
    belief1 = sent(belief1, low=1, of=(1,))
    part = call(
        functools.partial(third_kernel, offset),
        "third",
        arr(1, 2 * n + half),
        4,
        bufs + pair + [pltpu.VMEM((lines, LANES), F32)],
    )(place, rows, cols, seen)
    parts = [sent(part, core=j, high=k, of=(1,)) for j, k in ((1, 0), (0, 1), (1, 1))]
    return call(functools.partial(last_kernel, offset), "last", arr(1, n), 8)(
        place, potentials, belief1, rows, part, *parts
    )


def solution(mesh):
    return jax.shard_map(
        body,
        mesh=mesh,
        in_specs=(P("tm", None, "cell"), P("tm", "cell")),
        out_specs=P("tm", "cell"),
        check_vma=False,
    )
```

```python
import functools
import itertools
import math

import jax
import jax.numpy as jnp
from jax import lax
from jax.experimental import pallas as pl
from jax.experimental.pallas import tpu as pltpu
from jax.sharding import PartitionSpec as P

LOG2E = math.log2(math.e)
LN2 = math.log(2.0)
LANES = 128
VMEM_LIMIT = 50 * 2**20

F32 = jnp.float32
BF16 = jnp.bfloat16

PLACES = 8
CORNERS = 4


def params():
    return pltpu.CompilerParams(vmem_limit_bytes=VMEM_LIMIT)


def halves(x):
    high = x.astype(BF16)
    return high, (x - high.astype(F32)).astype(BF16)


def bias_rows(first, w, n):
    w1 = w.astype(BF16).astype(F32)
    w2 = (w - w1).astype(BF16).astype(F32)
    w3 = w - w1 - w2
    row = lax.broadcasted_iota(jnp.int32, (16, n), 0)
    other = 3 - first
    block = jnp.where(row == first, w1, jnp.where(row == first + 1, w2, jnp.where(row == first + 2, w3, 0.0)))
    block = jnp.where((row >= other) & (row < other + 3), 1.0, block)
    return jnp.concatenate([block.astype(BF16), jnp.zeros((48, n), BF16)], axis=0)


def row_side(x, w):
    high, low = halves(x * (2.0 * LOG2E))
    return jnp.concatenate([high, high, low, bias_rows(3, w, x.shape[1])], axis=0)


def col_side(x, w):
    high, low = halves(x)
    return jnp.concatenate([high, low, high, bias_rows(0, w, x.shape[1])], axis=0)


def square(x):
    return jnp.sum(x * x, axis=0, keepdims=True)


def largest(parts):
    return functools.reduce(jnp.maximum, parts)


def added(parts):
    while len(parts) > 1:
        parts = [functools.reduce(jnp.add, parts[i : i + 2]) for i in range(0, len(parts), 2)]
    return parts[0]


def lse2(parts):
    top = largest(parts)
    return top + jnp.log2(added([jnp.exp2(p - top) for p in parts]))


def times(a, b):
    return lax.dot_general(a, b, (((1,), (0,)), ((), ())), preferred_element_type=F32)


def piped(count, start, finish):
    start(0)
    for k in range(count):
        if k + 1 < count:
            start(k + 1)
        finish(k)


def more(state, parts):
    best = largest(parts)
    if state is None:
        return best, added([jnp.exp2(p - best) for p in parts])
    top, total = state
    new = jnp.maximum(top, best)
    return new, total * jnp.exp2(top - new) + added([jnp.exp2(p - new) for p in parts])


def over_columns(rows_t, col_chunk, chunks, width, bufs, top, total):
    n = rows_t.shape[0]
    step = 32

    def start(k):
        bufs[k % 2][...] = times(rows_t, col_chunk(k))

    def finish(k):
        buf = bufs[k % 2]
        for r in range(0, n, step):
            at = slice(r, r + step)
            state = None if k == 0 else (top[at, :], total[at, :])
            a, b = more(state, [buf[at, i : i + LANES] for i in range(0, width, LANES)])
            top[at, :] = a
            total[at, :] = b

    piped(chunks, start, finish)
    a = jnp.transpose(top[...])
    b = jnp.transpose(total[...])
    best = jnp.max(a, axis=0, keepdims=True)
    return best + jnp.log2(jnp.sum(b * jnp.exp2(a - best), axis=0, keepdims=True))


def over_rows(rows_t, col_chunk, chunks, width, bufs):
    n = rows_t.shape[0]
    step = 8
    lines = []

    def start(k):
        bufs[k % 2][:, 0:width] = times(rows_t, col_chunk(k))

    def finish(k):
        buf = bufs[k % 2]
        for i in range(0, width, LANES):
            state = None
            for r in range(0, n, 32 * step):
                state = more(state, [buf[q : q + step, i : i + LANES] for q in range(r, r + 32 * step, step)])
            a, b = state
            best = jnp.max(a, axis=0, keepdims=True)
            lines.append(best + jnp.log2(jnp.sum(b * jnp.exp2(a - best), axis=0, keepdims=True)))

    piped(chunks, start, finish)
    return lines


def pack_kernel(own, own_pot, out):
    dims = own.shape[1]
    out[0:dims, :] = own[0]
    out[dims:, :] = jnp.broadcast_to(own_pot[...], (8, own.shape[2]))


def spread_kernel(offset, place, own, other, other_pot, out, target, base, half_shard, sems):
    core = place[1]
    dims = other.shape[1]
    n = own.shape[1]
    half = n // 2
    at = pl.multiple_of(core * half, half)
    half_shard[0:dims, :] = jnp.where(core == 0, own[0:dims, pl.ds(at, half)], other[0, :, pl.ds(at, half)])
    half_shard[dims:, :] = jnp.where(
        core == 0, own[dims:, pl.ds(at, half)], jnp.broadcast_to(other_pot[:, pl.ds(at, half)], (8, half))
    )
    copies = [pltpu.make_async_copy(half_shard, out.at[i], sems.at[i]) for i in range(out.shape[0])]
    for c in copies:
        c.start()
    target[0:dims, :] = jnp.where(core == 0, other[0], own[0:dims, :])
    target[dims:, :] = jnp.where(core == 0, jnp.broadcast_to(other_pot[...], (8, n)), own[dims:, :])
    base[...] = own[dims : dims + 1, :] - square(own[0:dims, :]) - offset
    for c in copies:
        c.wait()


def order_kernel(place, own, other, out):
    n = own.shape[1]
    first = place[2] == 0
    out[:, 0:n] = jnp.where(first, own[...], other[...])
    out[:, n:] = jnp.where(first, other[...], own[...])


def first_kernel(place, rows, cols, *rest):
    *so_far, out, one, two, top, total = rest
    dims = rows.shape[0] - 8

    @pl.when(place[0] == 0)
    def _():
        y = rows[0:dims, :]
        rows_t = jnp.transpose(row_side(y, jnp.zeros((1, y.shape[1]), F32)))

        def chunk(k):
            parts = []
            for i in range(4 * k, 4 * k + 4):
                x = cols[i, 0:dims, :]
                parts.append(col_side(x, (cols[i, dims : dims + 1, :] - square(x)) * LOG2E))
            return jnp.concatenate(parts, axis=1)

        line = over_columns(rows_t, chunk, cols.shape[0] // 4, 4 * cols.shape[2], (one, two), top, total)
        out[...] = lse2([line] + [s[...] for s in so_far])

    @pl.when(place[0] != 0)
    def _():
        out[...] = jnp.zeros(out.shape, F32)


def second_kernel(offset, place, rows, near, far, *rest):
    *came, belief, out, one, two = rest
    dims = rows.shape[0] - 8
    blocks = near.shape[0]

    @pl.when(place[0] == 0)
    def _():
        belief[...] = jnp.zeros(belief.shape, F32)
        out[...] = jnp.zeros(out.shape, F32)

    @pl.when(place[0] != 0)
    def _():
        y = rows[0:dims, :]
        y2 = square(y)
        b = lse2([c[...] for c in came]) * LN2 - y2 - offset + rows[dims : dims + 1, :]
        n = b.shape[1] // 2
        belief[...] = jnp.where(place[2] == 0, b[:, 0:n], b[:, n:])
        rows_t = jnp.transpose(row_side(y, (b - y2) * LOG2E))

        def chunk(k):
            cols = near if k < blocks // 2 else far
            parts = []
            for i in (2 * k % blocks, 2 * k % blocks + 1):
                parts.append(col_side(cols[i, 0:dims, :], jnp.zeros((1, cols.shape[2]), F32)))
            return jnp.concatenate(parts, axis=1)

        lines = over_rows(rows_t, chunk, blocks, 2 * near.shape[2], (one, two))
        some = len(lines) // 2
        for k, side in enumerate((place[1], 1 - place[1])):
            block = jnp.concatenate(lines[k * some : (k + 1) * some], axis=0)
            at = pl.multiple_of(side * some, some)
            out[:, pl.ds(at, some), :] = jnp.broadcast_to(block[None], (out.shape[0], some, LANES))


def third_kernel(offset, place, rows, near, far, came, belief, out, one, two, top, total, seen, final):
    dims = rows.shape[0] - 8
    blocks = near.shape[0]
    some = 2 * blocks
    core = place[1]

    @pl.when(place[0] == 0)
    def _():
        out[...] = jnp.zeros(out.shape, F32)
        belief[...] = jnp.zeros(belief.shape, F32)

    @pl.when(place[0] != 0)
    def _():
        seen[...] = lse2([came[i] for i in range(came.shape[0])]) * LN2 - offset
        rows_t = jnp.transpose(row_side(rows[0:dims, :], jnp.zeros((1, rows.shape[1]), F32)))
        sides = [seen[pl.ds(pl.multiple_of(s * some, some), some), :] for s in (core, 1 - core)]

        def chunk(k):
            side = 0 if 4 * k < blocks else 1
            cols = (near, far)[side]
            parts = []
            for i in range(4 * k % blocks, 4 * k % blocks + 4):
                x = cols[i, 0:dims, :]
                x2 = square(x)
                lines = sides[side][2 * i : 2 * i + 2, :]
                b = jnp.concatenate([lines[0:1], lines[1:2]], axis=1) - x2 + cols[i, dims : dims + 1, :]
                final[side, i : i + 1, :] = b
                parts.append(col_side(x, (b - x2) * LOG2E))
            return jnp.concatenate(parts, axis=1)

        out[...] = over_columns(rows_t, chunk, blocks // 2, 4 * near.shape[2], (one, two), top, total)
        half = near.shape[2]
        mine, theirs = (final[side, pl.ds(place[4], 1), :] for side in (0, 1))
        belief[:, 0:half] = jnp.where(core == 0, mine, theirs)
        belief[:, half:] = jnp.where(core == 0, theirs, mine)


def last_kernel(place, pot, base, belief1, belief2, *rest):
    *came, out = rest
    here = 2 * place[0] + place[1]
    n = pot.shape[1]
    line = lse2([c[...] for c in came]) * LN2
    end = jnp.where(place[2] == 0, line[:, 0:n], line[:, n:]) + base[...]
    out[...] = jnp.where(here == 0, pot[...], jnp.where(here == 1, belief1[...], jnp.where(here == 2, belief2[...], end)))


def device(low, core, where, near, high):
    return ((low * 2 + core) * PLACES + where) * CORNERS + near * 2 + high


def moves(to):
    every = itertools.product((0, 1), (0, 1), range(PLACES), (0, 1), (0, 1))
    return [(device(*v), device(*to(*v))) for v in every]


def body(coords, potentials):
    _, dims, n = coords.shape
    cells = lax.axis_size("cell")
    offset = math.log(n * cells)
    tall = dims + 8
    half = n // 2
    here = lax.axis_index("tm")
    spot = lax.axis_index("cell")
    place = jnp.stack([here // 2, here % 2, spot % 2, spot // 2 % 2, spot // CORNERS]).astype(jnp.int32)
    smem = pl.BlockSpec(memory_space=pltpu.SMEM)
    vmem = pl.BlockSpec(memory_space=pltpu.VMEM)
    lines = 2 * PLACES * half // LANES

    def arr(*shape):
        return jax.ShapeDtypeStruct(shape, F32)

    def sent(x, to):
        return lax.ppermute(x, ("tm", "cell"), moves(to))

    def swapped(x):
        return sent(x, lambda l, c, p, y, h: (l, 1 - c, p, y, h))

    def call(kernel, name, out, ins, scratch=(), **kw):
        return pl.pallas_call(
            kernel,
            out_shape=out,
            in_specs=[smem] + [vmem] * (ins - 1),
            scratch_shapes=list(scratch),
            compiler_params=params(),
            name=name,
            **kw,
        )

    other = swapped(coords)
    other_pot = swapped(potentials)
    own = pl.pallas_call(pack_kernel, out_shape=arr(tall, n), compiler_params=params(), name="pack")(coords, potentials)
    copies, target, base = call(
        functools.partial(spread_kernel, offset),
        "spread",
        [arr(PLACES, tall, half), arr(tall, n), arr(1, n)],
        4,
        [pltpu.VMEM((tall, half), F32), pltpu.SemaphoreType.DMA((PLACES,))],
        out_specs=[pl.BlockSpec(memory_space=pl.ANY), vmem, vmem],
    )(place, own, other, other_pot)
    corners = [[p * CORNERS + k for p in range(PLACES)] for k in range(CORNERS)]
    near = lax.all_to_all(copies, "cell", 0, 0, axis_index_groups=corners, tiled=True)
    rows = call(order_kernel, "order", arr(tall, 2 * n), 3)(
        place,
        sent(target, lambda l, c, p, y, h: (l, y, p, c, h)),
        sent(target, lambda l, c, p, y, h: (l, y, p, c, 1 - h)),
    )
    near, rows = lax.optimization_barrier((near, rows))
    rows1 = sent(rows, lambda l, c, p, y, h: (1 - l, c, p, y, h))
    far = swapped(near)

    bufs = [pltpu.VMEM((2 * n, 4 * half), F32)] * 2
    pair = [pltpu.VMEM((2 * n, LANES), F32)] * 2
    part = call(first_kernel, "first", arr(1, 2 * n), 3, bufs + pair)(place, rows, near)
    part = call(first_kernel, "first_far", arr(1, 2 * n), 4, bufs + pair)(place, rows, far, part)
    parts = [
        sent(part, lambda l, c, p, y, h, j=j, k=k: (1 - l, c, p, y ^ j, h ^ k)) for j in (0, 1) for k in (0, 1)
    ]
    belief1, mine = call(
        functools.partial(second_kernel, offset), "second", [arr(1, n), arr(2 * PLACES, lines, LANES)], 8, bufs
    )(place, rows1, near, far, *parts)
    belief1 = sent(belief1, lambda l, c, p, y, h: (1 - l, c ^ y ^ 1, p, y, h))
    sixteen = [
        [device(l, c, p, y, h) for c in (0, 1) for p in range(PLACES)] for l in (0, 1) for y in (0, 1) for h in (0, 1)
    ]
    seen = lax.all_to_all(mine, ("tm", "cell"), 0, 0, axis_index_groups=sixteen, tiled=True)
    seen, belief1 = lax.optimization_barrier((seen, belief1))
    belief2, part = call(
        functools.partial(third_kernel, offset),
        "third",
        [arr(1, n), arr(1, 2 * n)],
        5,
        bufs + pair + [pltpu.VMEM((lines, LANES), F32), pltpu.VMEM((2, PLACES, half), F32)],
    )(place, rows, near, far, seen)
    parts = [
        sent(part, lambda l, c, p, y, h, j=j, k=k: (l, c ^ y ^ j ^ 1, p, y ^ j, h ^ k)) for j in (0, 1) for k in (0, 1)
    ]
    return call(last_kernel, "last", arr(1, n), 9)(place, potentials, base, belief1, belief2, *parts)


def solution(mesh):
    return jax.shard_map(
        body,
        mesh=mesh,
        in_specs=(P("tm", None, "cell"), P("tm", "cell")),
        out_specs=P("tm", "cell"),
        check_vma=False,
    )
```

```python
import functools
import itertools
import math

import jax
import jax.numpy as jnp
from jax import lax
from jax.experimental import pallas as pl
from jax.experimental.pallas import tpu as pltpu
from jax.sharding import PartitionSpec as P

LOG2E = math.log2(math.e)
LN2 = math.log(2.0)
LANES = 128
VMEM_LIMIT = 50 * 2**20

F32 = jnp.float32
BF16 = jnp.bfloat16

PLACES = 8
CORNERS = 4


def params():
    return pltpu.CompilerParams(vmem_limit_bytes=VMEM_LIMIT)


def halves(x):
    high = x.astype(BF16)
    return high, (x - high.astype(F32)).astype(BF16)


def bias_rows(first, w, n):
    w1 = w.astype(BF16).astype(F32)
    w2 = (w - w1).astype(BF16).astype(F32)
    w3 = w - w1 - w2
    row = lax.broadcasted_iota(jnp.int32, (16, n), 0)
    other = 3 - first
    block = jnp.where(row == first, w1, jnp.where(row == first + 1, w2, jnp.where(row == first + 2, w3, 0.0)))
    block = jnp.where((row >= other) & (row < other + 3), 1.0, block)
    return jnp.concatenate([block.astype(BF16), jnp.zeros((48, n), BF16)], axis=0)


def row_side(x, w):
    high, low = halves(x * (2.0 * LOG2E))
    return jnp.concatenate([high, high, low, bias_rows(3, w, x.shape[1])], axis=0)


def col_side(x, w):
    high, low = halves(x)
    return jnp.concatenate([high, low, high, bias_rows(0, w, x.shape[1])], axis=0)


def square(x):
    return jnp.sum(x * x, axis=0, keepdims=True)


def largest(parts):
    return functools.reduce(jnp.maximum, parts)


def added(parts):
    while len(parts) > 1:
        parts = [functools.reduce(jnp.add, parts[i : i + 2]) for i in range(0, len(parts), 2)]
    return parts[0]


def lse2(parts):
    top = largest(parts)
    return top + jnp.log2(added([jnp.exp2(p - top) for p in parts]))


def times(a, b):
    return lax.dot_general(a, b, (((1,), (0,)), ((), ())), preferred_element_type=F32)


def piped(count, start, finish):
    start(0)
    for k in range(count):
        if k + 1 < count:
            start(k + 1)
        finish(k)


def more(state, parts):
    best = largest(parts)
    if state is None:
        return best, added([jnp.exp2(p - best) for p in parts])
    top, total = state
    new = jnp.maximum(top, best)
    return new, total * jnp.exp2(top - new) + added([jnp.exp2(p - new) for p in parts])


def over_columns(rows_t, col_chunk, chunks, width, bufs, top, total):
    n = rows_t.shape[0]
    step = 32

    def start(k):
        bufs[k % 2][...] = times(rows_t, col_chunk(k))

    def finish(k):
        buf = bufs[k % 2]
        for r in range(0, n, step):
            at = slice(r, r + step)
            state = None if k == 0 else (top[at, :], total[at, :])
            a, b = more(state, [buf[at, i : i + LANES] for i in range(0, width, LANES)])
            top[at, :] = a
            total[at, :] = b

    piped(chunks, start, finish)
    a = jnp.transpose(top[...])
    b = jnp.transpose(total[...])
    best = jnp.max(a, axis=0, keepdims=True)
    return best + jnp.log2(jnp.sum(b * jnp.exp2(a - best), axis=0, keepdims=True))


def over_rows(rows_t, col_chunk, chunks, width, bufs):
    n = rows_t.shape[0]
    step = 8
    lines = []

    def start(k):
        bufs[k % 2][:, 0:width] = times(rows_t, col_chunk(k))

    def finish(k):
        buf = bufs[k % 2]
        for i in range(0, width, LANES):
            state = None
            for r in range(0, n, 32 * step):
                state = more(state, [buf[q : q + step, i : i + LANES] for q in range(r, r + 32 * step, step)])
            a, b = state
            best = jnp.max(a, axis=0, keepdims=True)
            lines.append(best + jnp.log2(jnp.sum(b * jnp.exp2(a - best), axis=0, keepdims=True)))

    piped(chunks, start, finish)
    return lines


def pack_kernel(own, own_pot, out, line, sems):
    dims, n = own.shape[1:]
    copies = [
        pltpu.make_async_copy(own.at[0], out.at[pl.ds(0, dims)], sems.at[0]),
        pltpu.make_async_copy(own_pot, line, sems.at[1]),
    ]
    for c in copies:
        c.start()
    for c in copies:
        c.wait()
    out[dims:, :] = jnp.broadcast_to(line[...], (8, n))


def spread_kernel(place, own, other, other_pot, out, half_shard, sems):
    core = place[1]
    dims = other.shape[1]
    half = own.shape[1] // 2
    at = pl.multiple_of(core * half, half)
    half_shard[0:dims, :] = jnp.where(core == 0, own[0:dims, pl.ds(at, half)], other[0, :, pl.ds(at, half)])
    half_shard[dims:, :] = jnp.where(
        core == 0, own[dims:, pl.ds(at, half)], jnp.broadcast_to(other_pot[:, pl.ds(at, half)], (8, half))
    )
    copies = [pltpu.make_async_copy(half_shard, out.at[i], sems.at[i]) for i in range(out.shape[0])]
    for c in copies:
        c.start()
    for c in copies:
        c.wait()


def order_kernel(offset, place, own, across, along, both, keep, give, base):
    dims = across.shape[1]
    n = own.shape[1]
    x = own[0:dims, :]
    base[...] = own[dims : dims + 1, :] - square(x) - offset
    for y_lo, out in ((1, keep), (0, give)):
        here = place[3] == y_lo
        mine = jnp.where(here, x, along[0])
        theirs = jnp.where(here, across[0], both[0])
        out[:, 0:n] = jnp.where(place[2] == 0, mine, theirs)
        out[:, n:] = jnp.where(place[2] == 0, theirs, mine)


def rows_kernel(place, keep, got, rows, operand):
    x = jnp.where(place[1] == 1, keep[...], got[...])
    rows[...] = x
    operand[...] = jnp.transpose(row_side(x, jnp.zeros((1, x.shape[1]), F32)))


def first_kernel(place, rows, cols, *rest):
    *so_far, out, one, two, top, total = rest
    dims = cols.shape[1] - 8
    n = rows.shape[0]

    @pl.when(place[0] == 0)
    def _():
        rows_t = rows[...]

        def chunk(k):
            parts = []
            for i in range(4 * k, 4 * k + 4):
                x = cols[i, 0:dims, :]
                parts.append(col_side(x, (cols[i, dims : dims + 1, :] - square(x)) * LOG2E))
            return jnp.concatenate(parts, axis=1)

        line = over_columns(rows_t, chunk, cols.shape[0] // 4, 4 * cols.shape[2], (one, two), top, total)
        if so_far:
            before, own_pot, other_pot = so_far
            line = lse2([line, before[...]])
            out[:, n:] = jnp.where(place[1] == 1, own_pot[...], other_pot[...])
        out[:, 0:n] = line

    @pl.when(place[0] != 0)
    def _():
        out[...] = jnp.zeros(out.shape, F32)


def second_kernel(offset, place, rows, near, far, *rest):
    *came, belief, out, one, two = rest
    dims, wide = rows.shape
    blocks = near.shape[0]

    @pl.when(place[0] == 0)
    def _():
        belief[...] = jnp.zeros(belief.shape, F32)
        out[...] = jnp.zeros(out.shape, F32)

    @pl.when(place[0] != 0)
    def _():
        y = rows[...]
        y2 = square(y)
        level = place[1] == place[3]
        pots = [jnp.where(level, came[k][:, wide:], came[2 + k][:, wide:]) for k in (0, 1)]
        first = place[2] == 0
        pot = jnp.concatenate([jnp.where(first, *pots), jnp.where(first, *pots[::-1])], axis=1)
        b = lse2([c[:, 0:wide] for c in came]) * LN2 - y2 - offset + pot
        n = wide // 2
        belief[...] = jnp.where(first, b[:, 0:n], b[:, n:])
        rows_t = jnp.transpose(row_side(y, (b - y2) * LOG2E))

        def chunk(k):
            cols = near if k < blocks // 2 else far
            parts = []
            for i in (2 * k % blocks, 2 * k % blocks + 1):
                parts.append(col_side(cols[i, 0:dims, :], jnp.zeros((1, cols.shape[2]), F32)))
            return jnp.concatenate(parts, axis=1)

        lines = over_rows(rows_t, chunk, blocks, 2 * near.shape[2], (one, two))
        some = len(lines) // 2
        for k, side in enumerate((place[1], 1 - place[1])):
            block = jnp.concatenate(lines[k * some : (k + 1) * some], axis=0)
            at = pl.multiple_of(side * some, some)
            out[:, pl.ds(at, some), :] = jnp.broadcast_to(block[None], (out.shape[0], some, LANES))


def third_kernel(offset, place, rows, near, far, came, belief, out, one, two, top, total, seen, final):
    dims = near.shape[1] - 8
    blocks = near.shape[0]
    some = 2 * blocks
    core = place[1]

    @pl.when(place[0] == 0)
    def _():
        out[...] = jnp.zeros(out.shape, F32)
        belief[...] = jnp.zeros(belief.shape, F32)

    @pl.when(place[0] != 0)
    def _():
        seen[...] = lse2([came[i] for i in range(came.shape[0])]) * LN2 - offset
        rows_t = rows[...]
        sides = [seen[pl.ds(pl.multiple_of(s * some, some), some), :] for s in (core, 1 - core)]

        def chunk(k):
            side = 0 if 4 * k < blocks else 1
            cols = (near, far)[side]
            parts = []
            for i in range(4 * k % blocks, 4 * k % blocks + 4):
                x = cols[i, 0:dims, :]
                x2 = square(x)
                lines = sides[side][2 * i : 2 * i + 2, :]
                b = jnp.concatenate([lines[0:1], lines[1:2]], axis=1) - x2 + cols[i, dims : dims + 1, :]
                final[side, i : i + 1, :] = b
                parts.append(col_side(x, (b - x2) * LOG2E))
            return jnp.concatenate(parts, axis=1)

        out[...] = over_columns(rows_t, chunk, blocks // 2, 4 * near.shape[2], (one, two), top, total)
        half = near.shape[2]
        mine, theirs = (final[side, pl.ds(place[4], 1), :] for side in (0, 1))
        belief[:, 0:half] = jnp.where(core == 0, mine, theirs)
        belief[:, half:] = jnp.where(core == 0, theirs, mine)


def last_kernel(place, pot, base, belief1, belief2, *rest):
    *came, out = rest
    here = 2 * place[0] + place[1]
    n = pot.shape[1]
    line = lse2([c[...] for c in came]) * LN2
    end = jnp.where(place[2] == 0, line[:, 0:n], line[:, n:]) + base[...]
    out[...] = jnp.where(here == 0, pot[...], jnp.where(here == 1, belief1[...], jnp.where(here == 2, belief2[...], end)))


def device(low, core, where, near, high):
    return ((low * 2 + core) * PLACES + where) * CORNERS + near * 2 + high


def moves(to):
    every = itertools.product((0, 1), (0, 1), range(PLACES), (0, 1), (0, 1))
    return [(device(*v), device(*to(*v))) for v in every]


def body(coords, potentials):
    _, dims, n = coords.shape
    cells = lax.axis_size("cell")
    offset = math.log(n * cells)
    tall = dims + 8
    half = n // 2
    here = lax.axis_index("tm")
    spot = lax.axis_index("cell")
    place = jnp.stack([here // 2, here % 2, spot % 2, spot // 2 % 2, spot // CORNERS]).astype(jnp.int32)
    smem = pl.BlockSpec(memory_space=pltpu.SMEM)
    vmem = pl.BlockSpec(memory_space=pltpu.VMEM)
    lines = 2 * PLACES * half // LANES

    def arr(*shape):
        return jax.ShapeDtypeStruct(shape, F32)

    def sent(x, to):
        return lax.ppermute(x, ("tm", "cell"), moves(to))

    def swapped(x):
        return sent(x, lambda l, c, p, y, h: (l, 1 - c, p, y, h))

    def call(kernel, name, out, ins, scratch=(), **kw):
        return pl.pallas_call(
            kernel,
            out_shape=out,
            in_specs=[smem] + [vmem] * (ins - 1),
            scratch_shapes=list(scratch),
            compiler_params=params(),
            name=name,
            **kw,
        )

    anywhere = pl.BlockSpec(memory_space=pl.ANY)
    other = swapped(coords)
    other_pot = swapped(potentials)
    corner = [
        sent(coords, lambda l, c, p, y, h, j=j, k=k: (l, c, p, y ^ j, h ^ k)) for j, k in ((0, 1), (1, 0), (1, 1))
    ]
    own = pl.pallas_call(
        pack_kernel,
        out_shape=arr(tall, n),
        in_specs=[anywhere, anywhere],
        scratch_shapes=[pltpu.VMEM((1, n), F32), pltpu.SemaphoreType.DMA((2,))],
        compiler_params=params(),
        name="pack",
    )(coords, potentials)
    copies = call(
        spread_kernel,
        "spread",
        arr(PLACES, tall, half),
        4,
        [pltpu.VMEM((tall, half), F32), pltpu.SemaphoreType.DMA((PLACES,))],
        out_specs=anywhere,
    )(place, own, other, other_pot)
    copies, *corner = lax.optimization_barrier((copies, *corner))
    corners = [[p * CORNERS + k for p in range(PLACES)] for k in range(CORNERS)]
    near = lax.all_to_all(copies, "cell", 0, 0, axis_index_groups=corners, tiled=True)
    keep, give, base = call(
        functools.partial(order_kernel, offset), "order", [arr(dims, 2 * n), arr(dims, 2 * n), arr(1, n)], 5
    )(place, own, *corner)
    rows, operand = call(
        rows_kernel, "rows", [arr(dims, 2 * n), jax.ShapeDtypeStruct((2 * n, 4 * dims), BF16)], 3
    )(place, keep, swapped(give))
    near, rows, operand = lax.optimization_barrier((near, rows, operand))
    rows1 = sent(rows, lambda l, c, p, y, h: (1 - l, c, p, y, h))
    far = swapped(near)

    bufs = [pltpu.VMEM((2 * n, 4 * half), F32)] * 2
    pair = [pltpu.VMEM((2 * n, LANES), F32)] * 2
    part = call(first_kernel, "first", arr(1, 2 * n), 3, bufs + pair)(place, operand, near)
    part = call(first_kernel, "first_far", arr(1, 3 * n), 6, bufs + pair)(
        place, operand, far, part, potentials, other_pot
    )
    parts = [
        sent(part, lambda l, c, p, y, h, j=j, k=k: (1 - l, c, p, y ^ j, h ^ k)) for j in (0, 1) for k in (0, 1)
    ]
    belief1, mine = call(
        functools.partial(second_kernel, offset), "second", [arr(1, n), arr(2 * PLACES, lines, LANES)], 8, bufs
    )(place, rows1, near, far, *parts)
    belief1 = sent(belief1, lambda l, c, p, y, h: (1 - l, c ^ y ^ 1, p, y, h))
    sixteen = [
        [device(l, c, p, y, h) for c in (0, 1) for p in range(PLACES)] for l in (0, 1) for y in (0, 1) for h in (0, 1)
    ]
    seen = lax.all_to_all(mine, ("tm", "cell"), 0, 0, axis_index_groups=sixteen, tiled=True)
    seen, belief1 = lax.optimization_barrier((seen, belief1))
    belief2, part = call(
        functools.partial(third_kernel, offset),
        "third",
        [arr(1, n), arr(1, 2 * n)],
        5,
        bufs + pair + [pltpu.VMEM((lines, LANES), F32), pltpu.VMEM((2, PLACES, half), F32)],
    )(place, operand, near, far, seen)
    parts = [
        sent(part, lambda l, c, p, y, h, j=j, k=k: (l, c ^ y ^ j ^ 1, p, y ^ j, h ^ k)) for j in (0, 1) for k in (0, 1)
    ]
    return call(last_kernel, "last", arr(1, n), 9)(place, potentials, base, belief1, belief2, *parts)


def solution(mesh):
    return jax.shard_map(
        body,
        mesh=mesh,
        in_specs=(P("tm", None, "cell"), P("tm", "cell")),
        out_specs=P("tm", "cell"),
        check_vma=False,
    )
```

```python
import functools
import itertools
import math

import jax
import jax.numpy as jnp
from jax import lax
from jax.experimental import pallas as pl
from jax.experimental.pallas import tpu as pltpu
from jax.sharding import PartitionSpec as P

LOG2E = math.log2(math.e)
LN2 = math.log(2.0)
LANES = 128
VMEM_LIMIT = 50 * 2**20

F32 = jnp.float32
BF16 = jnp.bfloat16

DEPTHS = 4
PLACES = 2 * DEPTHS


def params():
    return pltpu.CompilerParams(vmem_limit_bytes=VMEM_LIMIT)


def halves(x):
    high = x.astype(BF16)
    return high, (x - high.astype(F32)).astype(BF16)


def bias_rows(first, w, n):
    w1 = w.astype(BF16).astype(F32)
    w2 = (w - w1).astype(BF16).astype(F32)
    w3 = w - w1 - w2
    row = lax.broadcasted_iota(jnp.int32, (16, n), 0)
    other = 3 - first
    block = jnp.where(row == first, w1, jnp.where(row == first + 1, w2, jnp.where(row == first + 2, w3, 0.0)))
    block = jnp.where((row >= other) & (row < other + 3), 1.0, block)
    return jnp.concatenate([block.astype(BF16), jnp.zeros((48, n), BF16)], axis=0)


def row_side(x, w):
    high, low = halves(x * (2.0 * LOG2E))
    return jnp.concatenate([high, high, low, bias_rows(3, w, x.shape[1])], axis=0)


def col_side(x, w):
    high, low = halves(x)
    return jnp.concatenate([high, low, high, bias_rows(0, w, x.shape[1])], axis=0)


def square(x):
    return jnp.sum(x * x, axis=0, keepdims=True)


def largest(parts):
    return functools.reduce(jnp.maximum, parts)


def added(parts):
    while len(parts) > 1:
        parts = [functools.reduce(jnp.add, parts[i : i + 2]) for i in range(0, len(parts), 2)]
    return parts[0]


def lse2(parts):
    top = largest(parts)
    return top + jnp.log2(added([jnp.exp2(p - top) for p in parts]))


def times(a, b):
    return lax.dot_general(a, b, (((1,), (0,)), ((), ())), preferred_element_type=F32)


def piped(count, start, finish):
    start(0)
    for k in range(count):
        if k + 1 < count:
            start(k + 1)
        finish(k)


def more(state, parts):
    best = largest(parts)
    if state is None:
        return best, added([jnp.exp2(p - best) for p in parts])
    top, total = state
    new = jnp.maximum(top, best)
    return new, total * jnp.exp2(top - new) + added([jnp.exp2(p - new) for p in parts])


def over_columns(rows_t, col_chunk, chunks, width, bufs, top, total):
    n = rows_t.shape[0]
    step = 32

    def start(k):
        bufs[k % 2][...] = times(rows_t, col_chunk(k))

    def finish(k):
        buf = bufs[k % 2]
        for r in range(0, n, step):
            at = slice(r, r + step)
            state = None if k == 0 else (top[at, :], total[at, :])
            a, b = more(state, [buf[at, i : i + LANES] for i in range(0, width, LANES)])
            top[at, :] = a
            total[at, :] = b

    piped(chunks, start, finish)
    a = jnp.transpose(top[...])
    b = jnp.transpose(total[...])
    best = jnp.max(a, axis=0, keepdims=True)
    return best + jnp.log2(jnp.sum(b * jnp.exp2(a - best), axis=0, keepdims=True))


def over_rows(rows_t, col_chunk, chunks, width, bufs):
    n = rows_t.shape[0]
    step = 8
    lines = []

    def start(k):
        bufs[k % 2][:, 0:width] = times(rows_t, col_chunk(k))

    def finish(k):
        buf = bufs[k % 2]
        for i in range(0, width, LANES):
            state = None
            for r in range(0, n, 32 * step):
                state = more(state, [buf[q : q + step, i : i + LANES] for q in range(r, r + 32 * step, step)])
            a, b = state
            best = jnp.max(a, axis=0, keepdims=True)
            lines.append(best + jnp.log2(jnp.sum(b * jnp.exp2(a - best), axis=0, keepdims=True)))

    piped(chunks, start, finish)
    return lines


def pack_kernel(offset, own, own_pot, out, base):
    dims = own.shape[1]
    out[0:dims, :] = own[0]
    out[dims:, :] = jnp.broadcast_to(own_pot[...], (8, own.shape[2]))
    base[...] = own_pot[...] - square(own[0]) - offset


def pick_kernel(place, own, other, other_pot, source, target):
    first = place[1] == 0
    dims, n = other.shape[1:]
    theirs = jnp.concatenate([other[0], jnp.broadcast_to(other_pot[...], (8, n))], axis=0)
    source[...] = jnp.where(first, own[...], theirs)
    target[...] = jnp.where(first, theirs, own[...])


def order_kernel(place, own, other, out, operand):
    dims = own.shape[0] - 8
    n = own.shape[1]
    first = place[2] == 0
    out[:, 0:n] = jnp.where(first, own[...], other[...])
    out[:, n:] = jnp.where(first, other[...], own[...])
    operand[...] = jnp.transpose(row_side(out[0:dims, :], jnp.zeros((1, 2 * n), F32)))


def first_kernel(place, rows, *rest):
    *ins, out, one, two, top, total = rest
    cols, so_far = ins[:DEPTHS], ins[DEPTHS:]
    dims = cols[0].shape[0] - 8

    @pl.when(place[0] == 0)
    def _():
        def chunk(k):
            parts = []
            for c in cols[2 * k : 2 * k + 2]:
                x = c[0:dims, :]
                parts.append(col_side(x, (c[dims : dims + 1, :] - square(x)) * LOG2E))
            return jnp.concatenate(parts, axis=1)

        line = over_columns(rows[...], chunk, DEPTHS // 2, 2 * cols[0].shape[1], (one, two), top, total)
        out[...] = lse2([line] + [s[...] for s in so_far])

    @pl.when(place[0] != 0)
    def _():
        out[...] = jnp.zeros(out.shape, F32)


def split_kernel(place, *refs):
    *cols, out, extra = refs
    dims = cols[0].shape[0] - 8

    @pl.when(place[0] != 0)
    def _():
        for k, c in enumerate(cols):
            depth = lax.rem(place[4] + DEPTHS - k % DEPTHS, DEPTHS)
            high_y = lax.rem(place[5] + place[1] + k // DEPTHS, 2)
            at = 2 * depth + high_y
            x = c[0:dims, :]
            high, low = halves(x)
            out[at, :, :] = jnp.concatenate([high, low, high], axis=0)
            extra[at, 0:1, :] = square(x)
            extra[at, 1:2, :] = c[dims : dims + 1, :]


def second_kernel(offset, place, rows, cols, *rest):
    *came, belief, out, one, two = rest
    dims = rows.shape[0] - 8
    blocks, _, width = cols.shape

    @pl.when(place[0] == 0)
    def _():
        belief[...] = jnp.zeros(belief.shape, F32)
        out[...] = jnp.zeros(out.shape, F32)

    @pl.when(place[0] != 0)
    def _():
        y = rows[0:dims, :]
        y2 = square(y)
        b = lse2([c[...] for c in came]) * LN2 - y2 - offset + rows[dims : dims + 1, :]
        n = b.shape[1] // 2
        belief[...] = jnp.where(place[2] == 0, b[:, 0:n], b[:, n:])
        rows_t = jnp.transpose(row_side(y, (b - y2) * LOG2E))
        no_bias = bias_rows(0, jnp.zeros((1, width), F32), width)

        def chunk(k):
            return jnp.concatenate([cols[k], no_bias], axis=0)

        lines = over_rows(rows_t, chunk, blocks, width, (one, two))
        out[...] = jnp.broadcast_to(jnp.concatenate(lines, axis=0)[None], out.shape)


def third_kernel(offset, place, rows, cols, extra, came, belief, out, one, two, top, total, seen, final):
    blocks, _, width = cols.shape
    some = width // LANES

    @pl.when(place[0] == 0)
    def _():
        out[...] = jnp.zeros(out.shape, F32)
        belief[...] = jnp.zeros(belief.shape, F32)

    @pl.when(place[0] != 0)
    def _():
        seen[...] = lse2([came[i] for i in range(came.shape[0])]) * LN2 - offset

        def chunk(k):
            parts = []
            for i in (2 * k, 2 * k + 1):
                line = jnp.concatenate([seen[some * i + q : some * i + q + 1, :] for q in range(some)], axis=1)
                x2 = extra[i, 0:1, :]
                b = line - x2 + extra[i, 1:2, :]
                final[i : i + 1, :] = b
                parts.append(jnp.concatenate([cols[i], bias_rows(0, (b - x2) * LOG2E, width)], axis=0))
            return jnp.concatenate(parts, axis=1)

        out[...] = over_columns(rows[...], chunk, blocks // 2, 2 * width, (one, two), top, total)
        belief[...] = final[pl.ds(2 * place[4] + place[5], 1), :]


def last_kernel(place, pot, base, belief1, belief2, *rest):
    *came, out = rest
    here = 2 * place[0] + place[1]
    n = pot.shape[1]
    line = lse2([c[...] for c in came]) * LN2
    end = jnp.where(place[2] == 0, line[:, 0:n], line[:, n:]) + base[...]
    out[...] = jnp.where(here == 0, pot[...], jnp.where(here == 1, belief1[...], jnp.where(here == 2, belief2[...], end)))


def device(low, core, depth, far, near, high):
    return ((((low * 2 + core) * DEPTHS + depth) * 2 + far) * 2 + near) * 2 + high


def moves(to):
    every = itertools.product((0, 1), (0, 1), range(DEPTHS), (0, 1), (0, 1), (0, 1))
    return [(device(*v), device(*to(*v))) for v in every]


def body(coords, potentials):
    _, dims, n = coords.shape
    cells = lax.axis_size("cell")
    offset = math.log(n * cells)
    tall = dims + 8
    here = lax.axis_index("tm")
    spot = lax.axis_index("cell")
    place = jnp.stack([here // 2, here % 2, spot % 2, spot // 2 % 2, spot // 8, spot // 4 % 2]).astype(jnp.int32)
    smem = pl.BlockSpec(memory_space=pltpu.SMEM)
    vmem = pl.BlockSpec(memory_space=pltpu.VMEM)
    lines = PLACES * n // LANES

    def arr(*shape, dtype=F32):
        return jax.ShapeDtypeStruct(shape, dtype)

    def sent(x, to):
        return lax.ppermute(x, ("tm", "cell"), moves(to))

    def swapped(x):
        return sent(x, lambda l, c, z, f, y, h: (l, 1 - c, z, f, y, h))

    def call(kernel, name, out, ins, scratch=()):
        return pl.pallas_call(
            kernel,
            out_shape=out,
            in_specs=[smem] + [vmem] * (ins - 1),
            scratch_shapes=list(scratch),
            compiler_params=params(),
            name=name,
        )

    own, base = pl.pallas_call(
        functools.partial(pack_kernel, offset),
        out_shape=[arr(tall, n), arr(1, n)],
        compiler_params=params(),
        name="pack",
    )(coords, potentials)
    source, target = call(pick_kernel, "pick", [arr(tall, n)] * 2, 4)(
        place, own, swapped(coords), swapped(potentials)
    )
    sides = [
        sent(target, lambda l, c, z, f, y, h: (l, y, z, f, c, h)),
        sent(target, lambda l, c, z, f, y, h: (l, y, z, f, c, 1 - h)),
    ]
    near = [
        sent(source, lambda l, c, z, f, y, h, d=d: (l, c, (z + d) % DEPTHS, f ^ c, y, h)) for d in range(DEPTHS)
    ]
    rows, operand = call(order_kernel, "order", [arr(tall, 2 * n), arr(2 * n, 4 * dims, dtype=BF16)], 3)(place, *sides)
    rows1 = sent(rows, lambda l, c, z, f, y, h: (1 - l, c, z, f, y, h))
    far = [swapped(x) for x in near]

    bufs = [pltpu.VMEM((2 * n, 2 * n), F32)] * 2
    pair = [pltpu.VMEM((2 * n, LANES), F32)] * 2
    part = call(first_kernel, "first", arr(1, 2 * n), 6, bufs + pair)(place, operand, *near)
    part = call(first_kernel, "first_far", arr(1, 2 * n), 7, bufs + pair)(place, operand, *far, part)
    parts = [
        sent(part, lambda l, c, z, f, y, h, j=j, k=k: (1 - l, c, z, f, y ^ j, h ^ k)) for j in (0, 1) for k in (0, 1)
    ]
    cols, extra = call(
        split_kernel, "split", [arr(PLACES, 3 * dims, n, dtype=BF16), arr(PLACES, 8, n)], 1 + PLACES
    )(place, *near, *far)
    belief1, mine = call(
        functools.partial(second_kernel, offset), "second", [arr(1, n), arr(2 * PLACES, lines, LANES)], 7, bufs
    )(place, rows1, cols, *parts)
    belief1 = sent(belief1, lambda l, c, z, f, y, h: (1 - l, c ^ y ^ 1, z, f, y, h))
    sixteen = [
        [device(l, c, z, f, y, h) for c in (0, 1) for z in range(DEPTHS) for f in (0, 1)]
        for l in (0, 1)
        for y in (0, 1)
        for h in (0, 1)
    ]
    seen = lax.all_to_all(mine, ("tm", "cell"), 0, 0, axis_index_groups=sixteen, tiled=True)
    seen, belief1 = lax.optimization_barrier((seen, belief1))
    belief2, part = call(
        functools.partial(third_kernel, offset),
        "third",
        [arr(1, n), arr(1, 2 * n)],
        5,
        bufs + pair + [pltpu.VMEM((lines, LANES), F32), pltpu.VMEM((PLACES, n), F32)],
    )(place, operand, cols, extra, seen)
    parts = [
        sent(part, lambda l, c, z, f, y, h, j=j, k=k: (l, c ^ y ^ j ^ 1, z, f, y ^ j, h ^ k))
        for j in (0, 1)
        for k in (0, 1)
    ]
    return call(last_kernel, "last", arr(1, n), 9)(place, potentials, base, belief1, belief2, *parts)


def solution(mesh):
    return jax.shard_map(
        body,
        mesh=mesh,
        in_specs=(P("tm", None, "cell"), P("tm", "cell")),
        out_specs=P("tm", "cell"),
        check_vma=False,
    )
```

```python
import functools
import itertools
import math

import jax
import jax.numpy as jnp
from jax import lax
from jax.experimental import pallas as pl
from jax.experimental.pallas import tpu as pltpu
from jax.sharding import PartitionSpec as P

LOG2E = math.log2(math.e)
LN2 = math.log(2.0)
LANES = 128
VMEM_LIMIT = 50 * 2**20

F32 = jnp.float32
BF16 = jnp.bfloat16

DEPTHS = 4
PLACES = 2 * DEPTHS


def params():
    return pltpu.CompilerParams(vmem_limit_bytes=VMEM_LIMIT)


def halves(x):
    high = x.astype(BF16)
    return high, (x - high.astype(F32)).astype(BF16)


def bias_rows(first, w, n):
    w1 = w.astype(BF16).astype(F32)
    w2 = (w - w1).astype(BF16).astype(F32)
    w3 = w - w1 - w2
    row = lax.broadcasted_iota(jnp.int32, (16, n), 0)
    other = 3 - first
    block = jnp.where(row == first, w1, jnp.where(row == first + 1, w2, jnp.where(row == first + 2, w3, 0.0)))
    block = jnp.where((row >= other) & (row < other + 3), 1.0, block)
    return jnp.concatenate([block.astype(BF16), jnp.zeros((48, n), BF16)], axis=0)


def row_side(x, w):
    high, low = halves(x * (2.0 * LOG2E))
    return jnp.concatenate([high, high, low, bias_rows(3, w, x.shape[1])], axis=0)


def col_side(x, w):
    high, low = halves(x)
    return jnp.concatenate([high, low, high, bias_rows(0, w, x.shape[1])], axis=0)


def square(x):
    return jnp.sum(x * x, axis=0, keepdims=True)


def largest(parts):
    return functools.reduce(jnp.maximum, parts)


def added(parts):
    while len(parts) > 1:
        parts = [functools.reduce(jnp.add, parts[i : i + 2]) for i in range(0, len(parts), 2)]
    return parts[0]


def lse2(parts):
    top = largest(parts)
    return top + jnp.log2(added([jnp.exp2(p - top) for p in parts]))


def times(a, b):
    return lax.dot_general(a, b, (((1,), (0,)), ((), ())), preferred_element_type=F32)


def piped(count, start, finish):
    start(0)
    for k in range(count):
        if k + 1 < count:
            start(k + 1)
        finish(k)


def more(state, parts):
    best = largest(parts)
    if state is None:
        return best, added([jnp.exp2(p - best) for p in parts])
    top, total = state
    new = jnp.maximum(top, best)
    return new, total * jnp.exp2(top - new) + added([jnp.exp2(p - new) for p in parts])


def over_columns(rows_t, col_chunk, chunks, width, bufs, top, total):
    n = rows_t.shape[0]
    step = 32

    def start(k):
        bufs[k % 2][...] = times(rows_t, col_chunk(k))

    def finish(k):
        buf = bufs[k % 2]
        for r in range(0, n, step):
            at = slice(r, r + step)
            state = None if k == 0 else (top[at, :], total[at, :])
            a, b = more(state, [buf[at, i : i + LANES] for i in range(0, width, LANES)])
            top[at, :] = a
            total[at, :] = b

    piped(chunks, start, finish)
    a = jnp.transpose(top[...])
    b = jnp.transpose(total[...])
    best = jnp.max(a, axis=0, keepdims=True)
    return best + jnp.log2(jnp.sum(b * jnp.exp2(a - best), axis=0, keepdims=True))


def over_rows(rows_t, col_chunk, chunks, width, bufs):
    n = rows_t.shape[0]
    step = 8
    lines = []

    def start(k):
        bufs[k % 2][:, 0:width] = times(rows_t, col_chunk(k))

    def finish(k):
        buf = bufs[k % 2]
        for i in range(0, width, LANES):
            state = None
            for r in range(0, n, 32 * step):
                state = more(state, [buf[q : q + step, i : i + LANES] for q in range(r, r + 32 * step, step)])
            a, b = state
            best = jnp.max(a, axis=0, keepdims=True)
            lines.append(best + jnp.log2(jnp.sum(b * jnp.exp2(a - best), axis=0, keepdims=True)))

    piped(chunks, start, finish)
    return lines


def pack_kernel(offset, own, own_pot, out, base):
    dims = own.shape[1]
    out[0:dims, :] = own[0]
    out[dims:, :] = jnp.broadcast_to(own_pot[...], (8, own.shape[2]))
    base[...] = own_pot[...] - square(own[0]) - offset


def pick_kernel(place, own, other, other_pot, part, target):
    first = place[1] == 0
    dims, n = other.shape[1:]
    half = n // 2
    at = pl.multiple_of(place[1] * half, half)
    part[0:dims, :] = jnp.where(first, own[0:dims, pl.ds(at, half)], other[0, :, pl.ds(at, half)])
    part[dims:, :] = jnp.where(
        first, own[dims:, pl.ds(at, half)], jnp.broadcast_to(other_pot[:, pl.ds(at, half)], (8, half))
    )
    target[0:dims, :] = jnp.where(first, other[0], own[0:dims, :])
    target[dims:, :] = jnp.where(first, jnp.broadcast_to(other_pot[...], (8, n)), own[dims:, :])


def join_kernel(place, own, other, out):
    half = own.shape[1]
    first = place[5] == 0
    out[:, 0:half] = jnp.where(first, own[...], other[...])
    out[:, half:] = jnp.where(first, other[...], own[...])


def order_kernel(place, own, other, out, operand):
    dims = own.shape[0] - 8
    n = own.shape[1]
    first = place[2] == 0
    out[:, 0:n] = jnp.where(first, own[...], other[...])
    out[:, n:] = jnp.where(first, other[...], own[...])
    operand[...] = jnp.transpose(row_side(out[0:dims, :], jnp.zeros((1, 2 * n), F32)))


def first_kernel(place, rows, *rest):
    *ins, out, one, two, top, total = rest
    cols, so_far = ins[:DEPTHS], ins[DEPTHS:]
    dims = cols[0].shape[0] - 8

    @pl.when(place[0] == 0)
    def _():
        def chunk(k):
            parts = []
            for c in cols[2 * k : 2 * k + 2]:
                x = c[0:dims, :]
                parts.append(col_side(x, (c[dims : dims + 1, :] - square(x)) * LOG2E))
            return jnp.concatenate(parts, axis=1)

        line = over_columns(rows[...], chunk, DEPTHS // 2, 2 * cols[0].shape[1], (one, two), top, total)
        out[...] = lse2([line] + [s[...] for s in so_far])

    @pl.when(place[0] != 0)
    def _():
        out[...] = jnp.zeros(out.shape, F32)


def split_kernel(place, *refs):
    *cols, out, extra = refs
    dims = cols[0].shape[0] - 8

    @pl.when(place[0] != 0)
    def _():
        for k, c in enumerate(cols):
            depth = lax.rem(place[4] + DEPTHS - k % DEPTHS, DEPTHS)
            at = 2 * depth + lax.rem(place[1] + k // DEPTHS, 2)
            x = c[0:dims, :]
            high, low = halves(x)
            out[at, :, :] = jnp.concatenate([high, low, high], axis=0)
            extra[at, 0:1, :] = square(x)
            extra[at, 1:2, :] = c[dims : dims + 1, :]


def second_kernel(offset, place, rows, cols, *rest):
    *came, belief, out, one, two = rest
    dims = rows.shape[0] - 8
    blocks, _, width = cols.shape

    @pl.when(place[0] == 0)
    def _():
        belief[...] = jnp.zeros(belief.shape, F32)
        out[...] = jnp.zeros(out.shape, F32)

    @pl.when(place[0] != 0)
    def _():
        y = rows[0:dims, :]
        y2 = square(y)
        b = lse2([c[...] for c in came]) * LN2 - y2 - offset + rows[dims : dims + 1, :]
        n = b.shape[1] // 2
        belief[...] = jnp.where(place[2] == 0, b[:, 0:n], b[:, n:])
        rows_t = jnp.transpose(row_side(y, (b - y2) * LOG2E))
        no_bias = bias_rows(0, jnp.zeros((1, width), F32), width)

        def chunk(k):
            return jnp.concatenate([cols[k], no_bias], axis=0)

        lines = over_rows(rows_t, chunk, blocks, width, (one, two))
        out[...] = jnp.broadcast_to(jnp.concatenate(lines, axis=0)[None], out.shape)


def third_kernel(offset, place, rows, cols, extra, came, belief, out, one, two, top, total, seen, final):
    blocks, _, width = cols.shape
    some = width // LANES

    @pl.when(place[0] == 0)
    def _():
        out[...] = jnp.zeros(out.shape, F32)
        belief[...] = jnp.zeros(belief.shape, F32)

    @pl.when(place[0] != 0)
    def _():
        seen[...] = lse2([came[i] for i in range(came.shape[0])]) * LN2 - offset

        def chunk(k):
            parts = []
            for i in (2 * k, 2 * k + 1):
                line = jnp.concatenate([seen[some * i + q : some * i + q + 1, :] for q in range(some)], axis=1)
                x2 = extra[i, 0:1, :]
                b = line - x2 + extra[i, 1:2, :]
                final[i : i + 1, :] = b
                parts.append(jnp.concatenate([cols[i], bias_rows(0, (b - x2) * LOG2E, width)], axis=0))
            return jnp.concatenate(parts, axis=1)

        out[...] = over_columns(rows[...], chunk, blocks // 2, 2 * width, (one, two), top, total)
        half = width // 2
        for side in (0, 1):
            line = final[pl.ds(2 * place[4] + side, 1), :]
            belief[:, side * half : (side + 1) * half] = jnp.where(place[5] == 0, line[:, 0:half], line[:, half:])


def last_kernel(place, pot, base, belief1, belief2, *rest):
    *came, out = rest
    here = 2 * place[0] + place[1]
    n = pot.shape[1]
    line = lse2([c[...] for c in came]) * LN2
    end = jnp.where(place[2] == 0, line[:, 0:n], line[:, n:]) + base[...]
    out[...] = jnp.where(here == 0, pot[...], jnp.where(here == 1, belief1[...], jnp.where(here == 2, belief2[...], end)))


def device(low, core, depth, far, near, high):
    return ((((low * 2 + core) * DEPTHS + depth) * 2 + far) * 2 + near) * 2 + high


def moves(to):
    every = itertools.product((0, 1), (0, 1), range(DEPTHS), (0, 1), (0, 1), (0, 1))
    return [(device(*v), device(*to(*v))) for v in every]


def body(coords, potentials):
    _, dims, n = coords.shape
    cells = lax.axis_size("cell")
    offset = math.log(n * cells)
    tall = dims + 8
    here = lax.axis_index("tm")
    spot = lax.axis_index("cell")
    place = jnp.stack([here // 2, here % 2, spot % 2, spot // 2 % 2, spot // 8, spot // 4 % 2]).astype(jnp.int32)
    smem = pl.BlockSpec(memory_space=pltpu.SMEM)
    vmem = pl.BlockSpec(memory_space=pltpu.VMEM)
    lines = PLACES * n // LANES

    def arr(*shape, dtype=F32):
        return jax.ShapeDtypeStruct(shape, dtype)

    def sent(x, to):
        return lax.ppermute(x, ("tm", "cell"), moves(to))

    def swapped(x):
        return sent(x, lambda l, c, z, f, y, h: (l, 1 - c, z, f, y, h))

    def call(kernel, name, out, ins, scratch=()):
        return pl.pallas_call(
            kernel,
            out_shape=out,
            in_specs=[smem] + [vmem] * (ins - 1),
            scratch_shapes=list(scratch),
            compiler_params=params(),
            name=name,
        )

    own, base = pl.pallas_call(
        functools.partial(pack_kernel, offset),
        out_shape=[arr(tall, n), arr(1, n)],
        compiler_params=params(),
        name="pack",
    )(coords, potentials)
    half, target = call(pick_kernel, "pick", [arr(tall, n // 2), arr(tall, n)], 4)(
        place, own, swapped(coords), swapped(potentials)
    )
    sides = [
        sent(target, lambda l, c, z, f, y, h: (l, y, z, f, c, h)),
        sent(target, lambda l, c, z, f, y, h: (l, y, z, f, c, 1 - h)),
    ]
    joined = call(join_kernel, "join", arr(tall, n), 3)(
        place, half, sent(half, lambda l, c, z, f, y, h: (l, c, z, 1 - f, y, h))
    )
    near = [joined] + [
        sent(joined, lambda l, c, z, f, y, h, d=d: (l, c, (z + d) % DEPTHS, f, y, h)) for d in range(1, DEPTHS)
    ]
    rows, operand = call(order_kernel, "order", [arr(tall, 2 * n), arr(2 * n, 4 * dims, dtype=BF16)], 3)(place, *sides)
    rows1 = sent(rows, lambda l, c, z, f, y, h: (1 - l, c, z, f, y, h))
    far = [swapped(x) for x in near]

    bufs = [pltpu.VMEM((2 * n, 2 * n), F32)] * 2
    pair = [pltpu.VMEM((2 * n, LANES), F32)] * 2
    part = call(first_kernel, "first", arr(1, 2 * n), 6, bufs + pair)(place, operand, *near)
    part = call(first_kernel, "first_far", arr(1, 2 * n), 7, bufs + pair)(place, operand, *far, part)
    parts = [
        sent(part, lambda l, c, z, f, y, h, j=j, k=k: (1 - l, c, z, f, y ^ j, h ^ k)) for j in (0, 1) for k in (0, 1)
    ]
    cols, extra = call(
        split_kernel, "split", [arr(PLACES, 3 * dims, n, dtype=BF16), arr(PLACES, 8, n)], 1 + PLACES
    )(place, *near, *far)
    belief1, mine = call(
        functools.partial(second_kernel, offset), "second", [arr(1, n), arr(2 * PLACES, lines, LANES)], 7, bufs
    )(place, rows1, cols, *parts)
    belief1 = sent(belief1, lambda l, c, z, f, y, h: (1 - l, c ^ y ^ 1, z, f, y, h))
    sixteen = [
        [device(l, c, z, f, y, h) for c in (0, 1) for z in range(DEPTHS) for f in (0, 1)]
        for l in (0, 1)
        for y in (0, 1)
        for h in (0, 1)
    ]
    seen = lax.all_to_all(mine, ("tm", "cell"), 0, 0, axis_index_groups=sixteen, tiled=True)
    seen, belief1 = lax.optimization_barrier((seen, belief1))
    belief2, part = call(
        functools.partial(third_kernel, offset),
        "third",
        [arr(1, n), arr(1, 2 * n)],
        5,
        bufs + pair + [pltpu.VMEM((lines, LANES), F32), pltpu.VMEM((PLACES, n), F32)],
    )(place, operand, cols, extra, seen)
    parts = [
        sent(part, lambda l, c, z, f, y, h, j=j, k=k: (l, c ^ y ^ j ^ 1, z, f, y ^ j, h ^ k))
        for j in (0, 1)
        for k in (0, 1)
    ]
    return call(last_kernel, "last", arr(1, n), 9)(place, potentials, base, belief1, belief2, *parts)


def solution(mesh):
    return jax.shard_map(
        body,
        mesh=mesh,
        in_specs=(P("tm", None, "cell"), P("tm", "cell")),
        out_specs=P("tm", "cell"),
        check_vma=False,
    )
```

```python
import functools
import itertools
import math

import jax
import jax.numpy as jnp
from jax import lax
from jax.experimental import pallas as pl
from jax.experimental.pallas import tpu as pltpu
from jax.sharding import PartitionSpec as P

LOG2E = math.log2(math.e)
LN2 = math.log(2.0)
LANES = 128
VMEM_LIMIT = 50 * 2**20

F32 = jnp.float32
BF16 = jnp.bfloat16

DEPTHS = 4
PLACES = 2 * DEPTHS


def params():
    return pltpu.CompilerParams(vmem_limit_bytes=VMEM_LIMIT)


def halves(x):
    high = x.astype(BF16)
    return high, (x - high.astype(F32)).astype(BF16)


def bias_rows(first, w, n):
    w1 = w.astype(BF16).astype(F32)
    w2 = (w - w1).astype(BF16).astype(F32)
    w3 = w - w1 - w2
    row = lax.broadcasted_iota(jnp.int32, (16, n), 0)
    other = 3 - first
    block = jnp.where(row == first, w1, jnp.where(row == first + 1, w2, jnp.where(row == first + 2, w3, 0.0)))
    block = jnp.where((row >= other) & (row < other + 3), 1.0, block)
    return jnp.concatenate([block.astype(BF16), jnp.zeros((48, n), BF16)], axis=0)


def row_side(x, w):
    high, low = halves(x * (2.0 * LOG2E))
    return jnp.concatenate([high, high, low, bias_rows(3, w, x.shape[1])], axis=0)


def col_side(x, w):
    high, low = halves(x)
    return jnp.concatenate([high, low, high, bias_rows(0, w, x.shape[1])], axis=0)


def square(x):
    return jnp.sum(x * x, axis=0, keepdims=True)


def largest(parts):
    return functools.reduce(jnp.maximum, parts)


def added(parts):
    while len(parts) > 1:
        parts = [functools.reduce(jnp.add, parts[i : i + 2]) for i in range(0, len(parts), 2)]
    return parts[0]


def lse2(parts):
    top = largest(parts)
    return top + jnp.log2(added([jnp.exp2(p - top) for p in parts]))


def times(a, b):
    return lax.dot_general(a, b, (((1,), (0,)), ((), ())), preferred_element_type=F32)


def piped(count, start, finish):
    start(0)
    for k in range(count):
        if k + 1 < count:
            start(k + 1)
        finish(k)


def more(state, parts):
    best = largest(parts)
    if state is None:
        return best, added([jnp.exp2(p - best) for p in parts])
    top, total = state
    new = jnp.maximum(top, best)
    return new, total * jnp.exp2(top - new) + added([jnp.exp2(p - new) for p in parts])


def over_columns(rows_t, col_chunk, chunks, width, bufs, top, total):
    n = rows_t.shape[0]
    step = 32

    def start(k):
        bufs[k % 2][...] = times(rows_t, col_chunk(k))

    def finish(k):
        buf = bufs[k % 2]
        for r in range(0, n, step):
            at = slice(r, r + step)
            state = None if k == 0 else (top[at, :], total[at, :])
            a, b = more(state, [buf[at, i : i + LANES] for i in range(0, width, LANES)])
            top[at, :] = a
            total[at, :] = b

    piped(chunks, start, finish)
    a = jnp.transpose(top[...])
    b = jnp.transpose(total[...])
    best = jnp.max(a, axis=0, keepdims=True)
    return best + jnp.log2(jnp.sum(b * jnp.exp2(a - best), axis=0, keepdims=True))


def over_rows(rows_t, col_chunk, chunks, width, bufs):
    n = rows_t.shape[0]
    step = 8
    lines = []

    def start(k):
        bufs[k % 2][:, 0:width] = times(rows_t, col_chunk(k))

    def finish(k):
        buf = bufs[k % 2]
        for i in range(0, width, LANES):
            state = None
            for r in range(0, n, 32 * step):
                state = more(state, [buf[q : q + step, i : i + LANES] for q in range(r, r + 32 * step, step)])
            a, b = state
            best = jnp.max(a, axis=0, keepdims=True)
            lines.append(best + jnp.log2(jnp.sum(b * jnp.exp2(a - best), axis=0, keepdims=True)))

    piped(chunks, start, finish)
    return lines


def pack_kernel(offset, own, own_pot, out, base):
    dims = own.shape[1]
    out[0:dims, :] = own[0]
    out[dims:, :] = jnp.broadcast_to(own_pot[...], (8, own.shape[2]))
    base[...] = own_pot[...] - square(own[0]) - offset


def pick_kernel(place, own, other, other_pot, part, target):
    first = place[1] == 0
    dims, n = other.shape[1:]
    half = n // 2
    at = pl.multiple_of(place[1] * half, half)
    part[0:dims, :] = jnp.where(first, own[0:dims, pl.ds(at, half)], other[0, :, pl.ds(at, half)])
    part[dims:, :] = jnp.where(
        first, own[dims:, pl.ds(at, half)], jnp.broadcast_to(other_pot[:, pl.ds(at, half)], (8, half))
    )
    target[0:dims, :] = jnp.where(first, other[0], own[0:dims, :])
    target[dims:, :] = jnp.where(first, jnp.broadcast_to(other_pot[...], (8, n)), own[dims:, :])


def spread_kernel(part, out):
    out[...] = jnp.broadcast_to(part[...][None], out.shape)


def order_kernel(place, own, other, out, operand):
    dims = own.shape[0] - 8
    n = own.shape[1]
    first = place[2] == 0
    out[:, 0:n] = jnp.where(first, own[...], other[...])
    out[:, n:] = jnp.where(first, other[...], own[...])
    operand[...] = jnp.transpose(row_side(out[0:dims, :], jnp.zeros((1, 2 * n), F32)))


def first_kernel(place, rows, cols, *rest):
    *so_far, out, one, two, top, total = rest
    blocks, tall, width = cols.shape
    dims = tall - 8

    @pl.when(place[0] == 0)
    def _():
        def chunk(k):
            parts = []
            for i in range(4 * k, 4 * k + 4):
                x = cols[i, 0:dims, :]
                parts.append(col_side(x, (cols[i, dims : dims + 1, :] - square(x)) * LOG2E))
            return jnp.concatenate(parts, axis=1)

        line = over_columns(rows[...], chunk, blocks // 4, 4 * width, (one, two), top, total)
        out[...] = lse2([line] + [s[...] for s in so_far])

    @pl.when(place[0] != 0)
    def _():
        out[...] = jnp.zeros(out.shape, F32)


def split_kernel(place, near, far, out, extra):
    blocks, tall, _ = near.shape
    dims = tall - 8

    @pl.when(place[0] != 0)
    def _():
        for cols, side in ((near, place[1]), (far, 1 - place[1])):
            for i in range(blocks):
                at = side * blocks + i
                x = cols[i, 0:dims, :]
                high, low = halves(x)
                out[at, :, :] = jnp.concatenate([high, low, high], axis=0)
                extra[at, 0:1, :] = square(x)
                extra[at, 1:2, :] = cols[i, dims : dims + 1, :]


def second_kernel(offset, place, rows, cols, *rest):
    *came, belief, out, one, two = rest
    dims = rows.shape[0] - 8
    blocks, _, width = cols.shape

    @pl.when(place[0] == 0)
    def _():
        belief[...] = jnp.zeros(belief.shape, F32)
        out[...] = jnp.zeros(out.shape, F32)

    @pl.when(place[0] != 0)
    def _():
        y = rows[0:dims, :]
        y2 = square(y)
        b = lse2([c[...] for c in came]) * LN2 - y2 - offset + rows[dims : dims + 1, :]
        n = b.shape[1] // 2
        belief[...] = jnp.where(place[2] == 0, b[:, 0:n], b[:, n:])
        rows_t = jnp.transpose(row_side(y, (b - y2) * LOG2E))
        no_bias = bias_rows(0, jnp.zeros((1, width), F32), width)

        def chunk(k):
            return jnp.concatenate([jnp.concatenate([cols[i], no_bias], axis=0) for i in (2 * k, 2 * k + 1)], axis=1)

        lines = over_rows(rows_t, chunk, blocks // 2, 2 * width, (one, two))
        out[...] = jnp.broadcast_to(jnp.concatenate(lines, axis=0)[None], out.shape)


def third_kernel(offset, place, rows, cols, extra, came, before, belief, out, one, two, top, total, seen, final):
    blocks, _, width = cols.shape
    some = width // LANES

    @pl.when(place[0] == 0)
    def _():
        out[...] = jnp.zeros(out.shape, F32)
        belief[...] = jnp.zeros(belief.shape, F32)

    @pl.when(place[0] != 0)
    def _():
        seen[...] = lse2([came[i] for i in range(came.shape[0])]) * LN2 - offset

        def chunk(k):
            parts = []
            for i in range(4 * k, 4 * k + 4):
                line = jnp.concatenate([seen[some * i + q : some * i + q + 1, :] for q in range(some)], axis=1)
                x2 = extra[i, 0:1, :]
                b = line - x2 + extra[i, 1:2, :]
                final[i : i + 1, :] = b
                parts.append(jnp.concatenate([cols[i], bias_rows(0, (b - x2) * LOG2E, width)], axis=0))
            return jnp.concatenate(parts, axis=1)

        wide = rows.shape[0]
        out[:, 0:wide] = over_columns(rows[...], chunk, blocks // 4, 4 * width, (one, two), top, total)
        out[:, wide:] = before[...]
        own = 2 * place[4] + place[5]
        belief[:, 0:width] = final[pl.ds(own, 1), :]
        belief[:, width:] = final[pl.ds(own + blocks // 2, 1), :]


def last_kernel(place, pot, base, belief2, *rest):
    *came, out = rest
    here = 2 * place[0] + place[1]
    n = pot.shape[1]
    wide = 2 * n
    line = lse2([c[:, 0:wide] for c in came]) * LN2
    belief1 = came[0][:, wide:]
    end = jnp.where(place[2] == 0, line[:, 0:n], line[:, n:]) + base[...]
    out[...] = jnp.where(here == 0, pot[...], jnp.where(here == 1, belief1, jnp.where(here == 2, belief2[...], end)))


def device(low, core, depth, far, near, high):
    return ((((low * 2 + core) * DEPTHS + depth) * 2 + far) * 2 + near) * 2 + high


def moves(to):
    every = itertools.product((0, 1), (0, 1), range(DEPTHS), (0, 1), (0, 1), (0, 1))
    return [(device(*v), device(*to(*v))) for v in every]


def body(coords, potentials):
    _, dims, n = coords.shape
    cells = lax.axis_size("cell")
    offset = math.log(n * cells)
    tall = dims + 8
    here = lax.axis_index("tm")
    spot = lax.axis_index("cell")
    place = jnp.stack([here // 2, here % 2, spot % 2, spot // 2 % 2, spot // 8, spot // 4 % 2]).astype(jnp.int32)
    smem = pl.BlockSpec(memory_space=pltpu.SMEM)
    vmem = pl.BlockSpec(memory_space=pltpu.VMEM)
    lines = PLACES * n // LANES

    def arr(*shape, dtype=F32):
        return jax.ShapeDtypeStruct(shape, dtype)

    def sent(x, to):
        return lax.ppermute(x, ("tm", "cell"), moves(to))

    def swapped(x):
        return sent(x, lambda l, c, z, f, y, h: (l, 1 - c, z, f, y, h))

    def call(kernel, name, out, ins, scratch=()):
        return pl.pallas_call(
            kernel,
            out_shape=out,
            in_specs=[smem] + [vmem] * (ins - 1),
            scratch_shapes=list(scratch),
            compiler_params=params(),
            name=name,
        )

    own, base = pl.pallas_call(
        functools.partial(pack_kernel, offset),
        out_shape=[arr(tall, n), arr(1, n)],
        compiler_params=params(),
        name="pack",
    )(coords, potentials)
    half, target = call(pick_kernel, "pick", [arr(tall, n // 2), arr(tall, n)], 4)(
        place, own, swapped(coords), swapped(potentials)
    )
    sides = [
        sent(target, lambda l, c, z, f, y, h: (l, y, z, f, c, h)),
        sent(target, lambda l, c, z, f, y, h: (l, y, z, f, c, 1 - h)),
    ]
    copies = pl.pallas_call(
        spread_kernel, out_shape=arr(PLACES, tall, n // 2), compiler_params=params(), name="spread"
    )(half)
    rows, operand = call(order_kernel, "order", [arr(tall, 2 * n), arr(2 * n, 4 * dims, dtype=BF16)], 3)(place, *sides)
    copies, rows, operand = lax.optimization_barrier((copies, rows, operand))
    corners = [[p * 4 + k for p in range(PLACES)] for k in range(4)]
    near = lax.all_to_all(copies, "cell", 0, 0, axis_index_groups=corners, tiled=True)
    near, rows = lax.optimization_barrier((near, rows))
    rows1 = sent(rows, lambda l, c, z, f, y, h: (1 - l, c, z, f, y, h))
    far = swapped(near)

    bufs = [pltpu.VMEM((2 * n, 2 * n), F32)] * 2
    pair = [pltpu.VMEM((2 * n, LANES), F32)] * 2
    part = call(first_kernel, "first", arr(1, 2 * n), 3, bufs + pair)(place, operand, near)
    part = call(first_kernel, "first_far", arr(1, 2 * n), 4, bufs + pair)(place, operand, far, part)
    parts = [
        sent(part, lambda l, c, z, f, y, h, j=j, k=k: (1 - l, c, z, f, y ^ j, h ^ k)) for j in (0, 1) for k in (0, 1)
    ]
    cols, extra = call(
        split_kernel, "split", [arr(2 * PLACES, 3 * dims, n // 2, dtype=BF16), arr(2 * PLACES, 8, n // 2)], 3
    )(place, near, far)
    belief1, mine = call(
        functools.partial(second_kernel, offset), "second", [arr(1, n), arr(2 * PLACES, lines, LANES)], 7, bufs
    )(place, rows1, cols, *parts)
    sixteen = [
        [device(l, c, z, f, y, h) for c in (0, 1) for z in range(DEPTHS) for f in (0, 1)]
        for l in (0, 1)
        for y in (0, 1)
        for h in (0, 1)
    ]
    seen = lax.all_to_all(mine, ("tm", "cell"), 0, 0, axis_index_groups=sixteen, tiled=True)
    belief2, part = call(
        functools.partial(third_kernel, offset),
        "third",
        [arr(1, n), arr(1, 3 * n)],
        6,
        bufs + pair + [pltpu.VMEM((lines, LANES), F32), pltpu.VMEM((2 * PLACES, n // 2), F32)],
    )(place, operand, cols, extra, seen, belief1)

    def ending(l, c, z, f, y, h):
        return (l if c == y else 1 - l, l, z, f, c, h)

    parts = [sent(part, ending)] + [
        sent(part, lambda l, c, z, f, y, h, j=j, k=k: (l, c ^ y ^ j ^ 1, z, f, y ^ j, h ^ k))
        for j, k in ((0, 1), (1, 0), (1, 1))
    ]
    return call(last_kernel, "last", arr(1, n), 8)(place, potentials, base, belief2, *parts)


def solution(mesh):
    return jax.shard_map(
        body,
        mesh=mesh,
        in_specs=(P("tm", None, "cell"), P("tm", "cell")),
        out_specs=P("tm", "cell"),
        check_vma=False,
    )
```

```python
import functools
import itertools
import math

import jax
import jax.numpy as jnp
from jax import lax
from jax.experimental import pallas as pl
from jax.experimental.pallas import tpu as pltpu
from jax.sharding import PartitionSpec as P

LOG2E = math.log2(math.e)
LN2 = math.log(2.0)
LANES = 128
VMEM_LIMIT = 50 * 2**20

F32 = jnp.float32
BF16 = jnp.bfloat16

DEPTHS = 4
PLACES = 2 * DEPTHS


def params():
    return pltpu.CompilerParams(vmem_limit_bytes=VMEM_LIMIT)


def halves(x):
    high = x.astype(BF16)
    return high, (x - high.astype(F32)).astype(BF16)


def bias_rows(first, w, n):
    w1 = w.astype(BF16).astype(F32)
    w2 = (w - w1).astype(BF16).astype(F32)
    w3 = w - w1 - w2
    row = lax.broadcasted_iota(jnp.int32, (16, n), 0)
    other = 3 - first
    block = jnp.where(row == first, w1, jnp.where(row == first + 1, w2, jnp.where(row == first + 2, w3, 0.0)))
    block = jnp.where((row >= other) & (row < other + 3), 1.0, block)
    return jnp.concatenate([block.astype(BF16), jnp.zeros((48, n), BF16)], axis=0)


def row_side(x, w):
    high, low = halves(x * (2.0 * LOG2E))
    return jnp.concatenate([high, high, low, bias_rows(3, w, x.shape[1])], axis=0)


def col_side(x, w):
    high, low = halves(x)
    return jnp.concatenate([high, low, high, bias_rows(0, w, x.shape[1])], axis=0)


def square(x):
    return jnp.sum(x * x, axis=0, keepdims=True)


def largest(parts):
    return functools.reduce(jnp.maximum, parts)


def added(parts):
    while len(parts) > 1:
        parts = [functools.reduce(jnp.add, parts[i : i + 2]) for i in range(0, len(parts), 2)]
    return parts[0]


def lse2(parts):
    top = largest(parts)
    return top + jnp.log2(added([jnp.exp2(p - top) for p in parts]))


def times(a, b):
    return lax.dot_general(a, b, (((1,), (0,)), ((), ())), preferred_element_type=F32)


def piped(count, start, finish):
    start(0)
    for k in range(count):
        if k + 1 < count:
            start(k + 1)
        finish(k)


def more(state, parts):
    best = largest(parts)
    if state is None:
        return best, added([jnp.exp2(p - best) for p in parts])
    top, total = state
    new = jnp.maximum(top, best)
    return new, total * jnp.exp2(top - new) + added([jnp.exp2(p - new) for p in parts])


def over_columns(rows_t, col_chunk, chunks, width, bufs, top, total):
    n = rows_t.shape[0]
    step = 32

    def start(k):
        bufs[k % 2][...] = times(rows_t, col_chunk(k))

    def finish(k):
        buf = bufs[k % 2]
        for r in range(0, n, step):
            at = slice(r, r + step)
            state = None if k == 0 else (top[at, :], total[at, :])
            a, b = more(state, [buf[at, i : i + LANES] for i in range(0, width, LANES)])
            top[at, :] = a
            total[at, :] = b

    piped(chunks, start, finish)
    a = jnp.transpose(top[...])
    b = jnp.transpose(total[...])
    best = jnp.max(a, axis=0, keepdims=True)
    return best + jnp.log2(jnp.sum(b * jnp.exp2(a - best), axis=0, keepdims=True))


def over_rows(rows_t, col_chunk, chunks, width, bufs):
    n = rows_t.shape[0]
    step = 8
    lines = []

    def start(k):
        bufs[k % 2][:, 0:width] = times(rows_t, col_chunk(k))

    def finish(k):
        buf = bufs[k % 2]
        for i in range(0, width, LANES):
            state = None
            for r in range(0, n, 32 * step):
                state = more(state, [buf[q : q + step, i : i + LANES] for q in range(r, r + 32 * step, step)])
            a, b = state
            best = jnp.max(a, axis=0, keepdims=True)
            lines.append(best + jnp.log2(jnp.sum(b * jnp.exp2(a - best), axis=0, keepdims=True)))

    piped(chunks, start, finish)
    return lines


def pack_kernel(offset, own, own_pot, out, base):
    dims = own.shape[1]
    out[0:dims, :] = own[0]
    out[dims:, :] = jnp.broadcast_to(own_pot[...], (8, own.shape[2]))
    base[...] = own_pot[...] - square(own[0]) - offset


def pick_kernel(place, own, other, other_pot, part, target):
    first = place[1] == 0
    dims, n = other.shape[1:]
    half = n // 2
    at = pl.multiple_of(place[1] * half, half)
    part[0:dims, :] = jnp.where(first, own[0:dims, pl.ds(at, half)], other[0, :, pl.ds(at, half)])
    part[dims:, :] = jnp.where(
        first, own[dims:, pl.ds(at, half)], jnp.broadcast_to(other_pot[:, pl.ds(at, half)], (8, half))
    )
    target[0:dims, :] = jnp.where(first, other[0], own[0:dims, :])
    target[dims:, :] = jnp.where(first, jnp.broadcast_to(other_pot[...], (8, n)), own[dims:, :])


def spread_kernel(part, out):
    out[...] = jnp.broadcast_to(part[...][None], out.shape)


def order_kernel(place, own, other, out, operand):
    dims = own.shape[0] - 8
    n = own.shape[1]
    first = place[2] == 0
    out[:, 0:n] = jnp.where(first, own[...], other[...])
    out[:, n:] = jnp.where(first, other[...], own[...])
    operand[...] = jnp.transpose(row_side(out[0:dims, :], jnp.zeros((1, 2 * n), F32)))


def first_kernel(place, rows, cols, *rest):
    *so_far, out, one, two, top, total = rest
    blocks, tall, width = cols.shape
    dims = tall - 8

    @pl.when(place[0] == 0)
    def _():
        def chunk(k):
            parts = []
            for i in range(4 * k, 4 * k + 4):
                x = cols[i, 0:dims, :]
                parts.append(col_side(x, (cols[i, dims : dims + 1, :] - square(x)) * LOG2E))
            return jnp.concatenate(parts, axis=1)

        line = over_columns(rows[...], chunk, blocks // 4, 4 * width, (one, two), top, total)
        out[...] = lse2([line] + [s[...] for s in so_far])

    @pl.when(place[0] != 0)
    def _():
        out[...] = jnp.zeros(out.shape, F32)


def split_kernel(place, near, far, out, extra):
    blocks, tall, _ = near.shape
    dims = tall - 8

    @pl.when(place[0] != 0)
    def _():
        for cols, side in ((near, place[1]), (far, 1 - place[1])):
            for i in range(blocks):
                at = side * blocks + i
                x = cols[i, 0:dims, :]
                high, low = halves(x)
                out[at, :, :] = jnp.concatenate([high, low, high], axis=0)
                extra[at, 0:1, :] = square(x)
                extra[at, 1:2, :] = cols[i, dims : dims + 1, :]


def second_kernel(offset, place, rows, cols, *rest):
    *came, belief, out, one, two = rest
    dims = rows.shape[0] - 8
    blocks, _, width = cols.shape

    @pl.when(place[0] == 0)
    def _():
        belief[...] = jnp.zeros(belief.shape, F32)
        out[...] = jnp.zeros(out.shape, F32)

    @pl.when(place[0] != 0)
    def _():
        y = rows[0:dims, :]
        y2 = square(y)
        b = lse2([c[...] for c in came]) * LN2 - y2 - offset + rows[dims : dims + 1, :]
        n = b.shape[1] // 2
        belief[...] = jnp.where(place[2] == 0, b[:, 0:n], b[:, n:])
        rows_t = jnp.transpose(row_side(y, (b - y2) * LOG2E))
        no_bias = bias_rows(0, jnp.zeros((1, width), F32), width)

        def chunk(k):
            return jnp.concatenate([jnp.concatenate([cols[i], no_bias], axis=0) for i in (2 * k, 2 * k + 1)], axis=1)

        lines = over_rows(rows_t, chunk, blocks // 2, 2 * width, (one, two))
        out[...] = jnp.broadcast_to(jnp.concatenate(lines, axis=0)[None], out.shape)


def third_kernel(offset, place, rows, cols, extra, came, belief, out, one, two, top, total, seen, final):
    blocks, _, width = cols.shape
    some = width // LANES

    @pl.when(place[0] == 0)
    def _():
        out[...] = jnp.zeros(out.shape, F32)
        belief[...] = jnp.zeros(belief.shape, F32)

    @pl.when(place[0] != 0)
    def _():
        seen[...] = lse2([came[i] for i in range(came.shape[0])]) * LN2 - offset

        def chunk(k):
            parts = []
            for i in range(4 * k, 4 * k + 4):
                line = jnp.concatenate([seen[some * i + q : some * i + q + 1, :] for q in range(some)], axis=1)
                x2 = extra[i, 0:1, :]
                b = line - x2 + extra[i, 1:2, :]
                final[i : i + 1, :] = b
                parts.append(jnp.concatenate([cols[i], bias_rows(0, (b - x2) * LOG2E, width)], axis=0))
            return jnp.concatenate(parts, axis=1)

        out[...] = over_columns(rows[...], chunk, blocks // 4, 4 * width, (one, two), top, total)
        own = 2 * place[4] + place[5]
        belief[:, 0:width] = final[pl.ds(own, 1), :]
        belief[:, width:] = final[pl.ds(own + blocks // 2, 1), :]


def last_kernel(place, pot, base, belief1, belief2, *rest):
    *came, out = rest
    here = 2 * place[0] + place[1]
    n = pot.shape[1]
    line = lse2([c[...] for c in came]) * LN2
    end = jnp.where(place[2] == 0, line[:, 0:n], line[:, n:]) + base[...]
    out[...] = jnp.where(here == 0, pot[...], jnp.where(here == 1, belief1[...], jnp.where(here == 2, belief2[...], end)))


def device(low, core, depth, far, near, high):
    return ((((low * 2 + core) * DEPTHS + depth) * 2 + far) * 2 + near) * 2 + high


def moves(to):
    every = itertools.product((0, 1), (0, 1), range(DEPTHS), (0, 1), (0, 1), (0, 1))
    return [(device(*v), device(*to(*v))) for v in every]


def body(coords, potentials):
    _, dims, n = coords.shape
    cells = lax.axis_size("cell")
    offset = math.log(n * cells)
    tall = dims + 8
    here = lax.axis_index("tm")
    spot = lax.axis_index("cell")
    place = jnp.stack([here // 2, here % 2, spot % 2, spot // 2 % 2, spot // 8, spot // 4 % 2]).astype(jnp.int32)
    smem = pl.BlockSpec(memory_space=pltpu.SMEM)
    vmem = pl.BlockSpec(memory_space=pltpu.VMEM)
    lines = PLACES * n // LANES

    def arr(*shape, dtype=F32):
        return jax.ShapeDtypeStruct(shape, dtype)

    def sent(x, to):
        return lax.ppermute(x, ("tm", "cell"), moves(to))

    def swapped(x):
        return sent(x, lambda l, c, z, f, y, h: (l, 1 - c, z, f, y, h))

    def call(kernel, name, out, ins, scratch=()):
        return pl.pallas_call(
            kernel,
            out_shape=out,
            in_specs=[smem] + [vmem] * (ins - 1),
            scratch_shapes=list(scratch),
            compiler_params=params(),
            name=name,
        )

    own, base = pl.pallas_call(
        functools.partial(pack_kernel, offset),
        out_shape=[arr(tall, n), arr(1, n)],
        compiler_params=params(),
        name="pack",
    )(coords, potentials)
    half, target = call(pick_kernel, "pick", [arr(tall, n // 2), arr(tall, n)], 4)(
        place, own, swapped(coords), swapped(potentials)
    )
    sides = [
        sent(target, lambda l, c, z, f, y, h: (l, y, z, f, c, h)),
        sent(target, lambda l, c, z, f, y, h: (l, y, z, f, c, 1 - h)),
    ]
    copies = pl.pallas_call(
        spread_kernel, out_shape=arr(PLACES, tall, n // 2), compiler_params=params(), name="spread"
    )(half)
    rows, operand = call(order_kernel, "order", [arr(tall, 2 * n), arr(2 * n, 4 * dims, dtype=BF16)], 3)(place, *sides)
    corners = [[p * 4 + k for p in range(PLACES)] for k in range(4)]
    near = lax.all_to_all(copies, "cell", 0, 0, axis_index_groups=corners, tiled=True)
    near, rows = lax.optimization_barrier((near, rows))
    rows1 = sent(rows, lambda l, c, z, f, y, h: (1 - l, c, z, f, y, h))
    far = swapped(near)

    bufs = [pltpu.VMEM((2 * n, 2 * n), F32)] * 2
    pair = [pltpu.VMEM((2 * n, LANES), F32)] * 2
    part = call(first_kernel, "first", arr(1, 2 * n), 3, bufs + pair)(place, operand, near)
    part = call(first_kernel, "first_far", arr(1, 2 * n), 4, bufs + pair)(place, operand, far, part)
    parts = [
        sent(part, lambda l, c, z, f, y, h, j=j, k=k: (1 - l, c, z, f, y ^ j, h ^ k)) for j in (0, 1) for k in (0, 1)
    ]
    cols, extra = call(
        split_kernel, "split", [arr(2 * PLACES, 3 * dims, n // 2, dtype=BF16), arr(2 * PLACES, 8, n // 2)], 3
    )(place, near, far)
    belief1, mine = call(
        functools.partial(second_kernel, offset), "second", [arr(1, n), arr(2 * PLACES, lines, LANES)], 7, bufs
    )(place, rows1, cols, *parts)
    sixteen = [
        [device(l, c, z, f, y, h) for c in (0, 1) for z in range(DEPTHS) for f in (0, 1)]
        for l in (0, 1)
        for y in (0, 1)
        for h in (0, 1)
    ]
    seen = lax.all_to_all(mine, ("tm", "cell"), 0, 0, axis_index_groups=sixteen, tiled=True)
    seen, belief1 = lax.optimization_barrier((seen, belief1))
    belief1 = sent(belief1, lambda l, c, z, f, y, h: (1 - l, c ^ y ^ 1, z, f, y, h))
    belief2, part = call(
        functools.partial(third_kernel, offset),
        "third",
        [arr(1, n), arr(1, 2 * n)],
        5,
        bufs + pair + [pltpu.VMEM((lines, LANES), F32), pltpu.VMEM((2 * PLACES, n // 2), F32)],
    )(place, operand, cols, extra, seen)
    part, belief1 = lax.optimization_barrier((part, belief1))
    parts = [
        sent(part, lambda l, c, z, f, y, h, j=j, k=k: (l, c ^ y ^ j ^ 1, z, f, y ^ j, h ^ k))
        for j in (0, 1)
        for k in (0, 1)
    ]
    return call(last_kernel, "last", arr(1, n), 9)(place, potentials, base, belief1, belief2, *parts)


def solution(mesh):
    return jax.shard_map(
        body,
        mesh=mesh,
        in_specs=(P("tm", None, "cell"), P("tm", "cell")),
        out_specs=P("tm", "cell"),
        check_vma=False,
    )
```

```python
import functools
import itertools
import math

import jax
import jax.numpy as jnp
from jax import lax
from jax.experimental import pallas as pl
from jax.experimental.pallas import tpu as pltpu
from jax.sharding import PartitionSpec as P

LOG2E = math.log2(math.e)
LN2 = math.log(2.0)
LANES = 128
VMEM_LIMIT = 50 * 2**20

F32 = jnp.float32
BF16 = jnp.bfloat16

DEPTHS = 4
PLACES = 2 * DEPTHS


def params():
    return pltpu.CompilerParams(vmem_limit_bytes=VMEM_LIMIT)


def halves(x):
    high = x.astype(BF16)
    return high, (x - high.astype(F32)).astype(BF16)


def bias_rows(first, w, n):
    w1 = w.astype(BF16).astype(F32)
    w2 = (w - w1).astype(BF16).astype(F32)
    w3 = w - w1 - w2
    row = lax.broadcasted_iota(jnp.int32, (16, n), 0)
    other = 3 - first
    block = jnp.where(row == first, w1, jnp.where(row == first + 1, w2, jnp.where(row == first + 2, w3, 0.0)))
    block = jnp.where((row >= other) & (row < other + 3), 1.0, block)
    return jnp.concatenate([block.astype(BF16), jnp.zeros((48, n), BF16)], axis=0)


def row_side(x, w):
    high, low = halves(x * (2.0 * LOG2E))
    return jnp.concatenate([high, high, low, bias_rows(3, w, x.shape[1])], axis=0)


def col_side(x, w):
    high, low = halves(x)
    return jnp.concatenate([high, low, high, bias_rows(0, w, x.shape[1])], axis=0)


def square(x):
    return jnp.sum(x * x, axis=0, keepdims=True)


def largest(parts):
    return functools.reduce(jnp.maximum, parts)


def added(parts):
    while len(parts) > 1:
        parts = [functools.reduce(jnp.add, parts[i : i + 2]) for i in range(0, len(parts), 2)]
    return parts[0]


def lse2(parts):
    top = largest(parts)
    return top + jnp.log2(added([jnp.exp2(p - top) for p in parts]))


def times(a, b):
    return lax.dot_general(a, b, (((1,), (0,)), ((), ())), preferred_element_type=F32)


def piped(count, start, finish):
    start(0)
    for k in range(count):
        if k + 1 < count:
            start(k + 1)
        finish(k)


def more(state, parts):
    best = largest(parts)
    if state is None:
        return best, added([jnp.exp2(p - best) for p in parts])
    top, total = state
    new = jnp.maximum(top, best)
    return new, total * jnp.exp2(top - new) + added([jnp.exp2(p - new) for p in parts])


def over_columns(rows_t, col_chunk, chunks, width, bufs, top, total):
    n = rows_t.shape[0]
    step = 32

    def start(k):
        bufs[k % 2][:, 0:width] = times(rows_t, col_chunk(k))

    def finish(k):
        buf = bufs[k % 2]
        for r in range(0, n, step):
            at = slice(r, r + step)
            state = None if k == 0 else (top[at, :], total[at, :])
            a, b = more(state, [buf[at, i : i + LANES] for i in range(0, width, LANES)])
            top[at, :] = a
            total[at, :] = b

    piped(chunks, start, finish)
    a = jnp.transpose(top[...])
    b = jnp.transpose(total[...])
    best = jnp.max(a, axis=0, keepdims=True)
    return best + jnp.log2(jnp.sum(b * jnp.exp2(a - best), axis=0, keepdims=True))


def over_rows(rows_t, col_chunk, chunks, width, bufs):
    n = rows_t.shape[0]
    step = 8
    lines = []

    def start(k):
        bufs[k % 2][:, 0:width] = times(rows_t, col_chunk(k))

    def finish(k):
        buf = bufs[k % 2]
        for i in range(0, width, LANES):
            state = None
            for r in range(0, n, 32 * step):
                state = more(state, [buf[q : q + step, i : i + LANES] for q in range(r, r + 32 * step, step)])
            a, b = state
            best = jnp.max(a, axis=0, keepdims=True)
            lines.append(best + jnp.log2(jnp.sum(b * jnp.exp2(a - best), axis=0, keepdims=True)))

    piped(chunks, start, finish)
    return lines


def pack_kernel(offset, own, own_pot, out, base):
    dims = own.shape[1]
    out[0:dims, :] = own[0]
    out[dims:, :] = jnp.broadcast_to(own_pot[...], (8, own.shape[2]))
    base[...] = own_pot[...] - square(own[0]) - offset


def pick_kernel(place, own, other, other_pot, part, target):
    first = place[1] == 0
    dims, n = other.shape[1:]
    half = n // 2
    at = pl.multiple_of(place[1] * half, half)
    part[0:dims, :] = jnp.where(first, own[0:dims, pl.ds(at, half)], other[0, :, pl.ds(at, half)])
    part[dims:, :] = jnp.where(
        first, own[dims:, pl.ds(at, half)], jnp.broadcast_to(other_pot[:, pl.ds(at, half)], (8, half))
    )
    target[0:dims, :] = jnp.where(first, other[0], own[0:dims, :])
    target[dims:, :] = jnp.where(first, jnp.broadcast_to(other_pot[...], (8, n)), own[dims:, :])


def spread_kernel(part, out):
    out[...] = jnp.broadcast_to(part[...][None], out.shape)


def order_kernel(place, own, other, out, operand):
    dims = own.shape[0] - 8
    n = own.shape[1]
    first = place[2] == 0
    out[:, 0:n] = jnp.where(first, own[...], other[...])
    out[:, n:] = jnp.where(first, other[...], own[...])
    operand[...] = jnp.transpose(row_side(out[0:dims, :], jnp.zeros((1, 2 * n), F32)))


def first_kernel(place, rows, cols, *rest):
    *so_far, out, one, two, top, total = rest
    blocks, tall, width = cols.shape
    dims = tall - 8

    @pl.when(place[0] == 0)
    def _():
        def chunk(k):
            parts = []
            for i in range(2 * k, 2 * k + 2):
                x = cols[i, 0:dims, :]
                parts.append(col_side(x, (cols[i, dims : dims + 1, :] - square(x)) * LOG2E))
            return jnp.concatenate(parts, axis=1)

        line = over_columns(rows[...], chunk, blocks // 2, 2 * width, (one, two), top, total)
        out[...] = lse2([line] + [s[...] for s in so_far])

    @pl.when(place[0] != 0)
    def _():
        out[...] = jnp.zeros(out.shape, F32)


def split_kernel(place, near, far, out, extra):
    blocks, tall, _ = near.shape
    dims = tall - 8

    @pl.when(place[0] != 0)
    def _():
        for cols, side in ((near, place[1]), (far, 1 - place[1])):
            for i in range(blocks):
                at = side * blocks + i
                x = cols[i, 0:dims, :]
                high, low = halves(x)
                out[at, :, :] = jnp.concatenate([high, low, high], axis=0)
                extra[at, 0:1, :] = square(x)
                extra[at, 1:2, :] = cols[i, dims : dims + 1, :]


def second_kernel(offset, place, rows, cols, *rest):
    *came, belief, out, one, two = rest
    dims = rows.shape[0] - 8
    blocks, _, width = cols.shape

    @pl.when(place[0] == 0)
    def _():
        belief[...] = jnp.zeros(belief.shape, F32)
        out[...] = jnp.zeros(out.shape, F32)

    @pl.when(place[0] != 0)
    def _():
        y = rows[0:dims, :]
        y2 = square(y)
        b = lse2([c[...] for c in came]) * LN2 - y2 - offset + rows[dims : dims + 1, :]
        n = b.shape[1] // 2
        belief[...] = jnp.where(place[2] == 0, b[:, 0:n], b[:, n:])
        rows_t = jnp.transpose(row_side(y, (b - y2) * LOG2E))
        no_bias = bias_rows(0, jnp.zeros((1, width), F32), width)

        def chunk(k):
            return jnp.concatenate([jnp.concatenate([cols[i], no_bias], axis=0) for i in (2 * k, 2 * k + 1)], axis=1)

        lines = over_rows(rows_t, chunk, blocks // 2, 2 * width, (one, two))
        out[...] = jnp.broadcast_to(jnp.concatenate(lines, axis=0)[None], out.shape)


def third_kernel(offset, place, rows, cols, extra, came, belief, out, one, two, top, total, seen, final):
    blocks, _, width = cols.shape
    some = width // LANES

    @pl.when(place[0] == 0)
    def _():
        out[...] = jnp.zeros(out.shape, F32)
        belief[...] = jnp.zeros(belief.shape, F32)

    @pl.when(place[0] != 0)
    def _():
        seen[...] = lse2([came[i] for i in range(came.shape[0])]) * LN2 - offset

        def chunk(k):
            parts = []
            for i in range(4 * k, 4 * k + 4):
                line = jnp.concatenate([seen[some * i + q : some * i + q + 1, :] for q in range(some)], axis=1)
                x2 = extra[i, 0:1, :]
                b = line - x2 + extra[i, 1:2, :]
                final[i : i + 1, :] = b
                parts.append(jnp.concatenate([cols[i], bias_rows(0, (b - x2) * LOG2E, width)], axis=0))
            return jnp.concatenate(parts, axis=1)

        out[...] = over_columns(rows[...], chunk, blocks // 4, 4 * width, (one, two), top, total)
        own = 2 * place[4] + place[5]
        belief[:, 0:width] = final[pl.ds(own, 1), :]
        belief[:, width:] = final[pl.ds(own + blocks // 2, 1), :]


def last_kernel(place, pot, base, belief1, belief2, *rest):
    *came, out = rest
    here = 2 * place[0] + place[1]
    n = pot.shape[1]
    line = lse2([c[...] for c in came]) * LN2
    end = jnp.where(place[2] == 0, line[:, 0:n], line[:, n:]) + base[...]
    out[...] = jnp.where(here == 0, pot[...], jnp.where(here == 1, belief1[...], jnp.where(here == 2, belief2[...], end)))


def device(low, core, depth, far, near, high):
    return ((((low * 2 + core) * DEPTHS + depth) * 2 + far) * 2 + near) * 2 + high


def moves(to):
    every = itertools.product((0, 1), (0, 1), range(DEPTHS), (0, 1), (0, 1), (0, 1))
    return [(device(*v), device(*to(*v))) for v in every]


def body(coords, potentials):
    _, dims, n = coords.shape
    cells = lax.axis_size("cell")
    offset = math.log(n * cells)
    tall = dims + 8
    here = lax.axis_index("tm")
    spot = lax.axis_index("cell")
    place = jnp.stack([here // 2, here % 2, spot % 2, spot // 2 % 2, spot // 8, spot // 4 % 2]).astype(jnp.int32)
    smem = pl.BlockSpec(memory_space=pltpu.SMEM)
    vmem = pl.BlockSpec(memory_space=pltpu.VMEM)
    lines = PLACES * n // LANES

    def arr(*shape, dtype=F32):
        return jax.ShapeDtypeStruct(shape, dtype)

    def sent(x, to):
        return lax.ppermute(x, ("tm", "cell"), moves(to))

    def swapped(x):
        return sent(x, lambda l, c, z, f, y, h: (l, 1 - c, z, f, y, h))

    def call(kernel, name, out, ins, scratch=()):
        return pl.pallas_call(
            kernel,
            out_shape=out,
            in_specs=[smem] + [vmem] * (ins - 1),
            scratch_shapes=list(scratch),
            compiler_params=params(),
            name=name,
        )

    own, base = pl.pallas_call(
        functools.partial(pack_kernel, offset),
        out_shape=[arr(tall, n), arr(1, n)],
        compiler_params=params(),
        name="pack",
    )(coords, potentials)
    half, target = call(pick_kernel, "pick", [arr(tall, n // 2), arr(tall, n)], 4)(
        place, own, swapped(coords), swapped(potentials)
    )
    sides = [
        sent(target, lambda l, c, z, f, y, h: (l, y, z, f, c, h)),
        sent(target, lambda l, c, z, f, y, h: (l, y, z, f, c, 1 - h)),
    ]
    copies = pl.pallas_call(
        spread_kernel, out_shape=arr(PLACES, tall, n // 2), compiler_params=params(), name="spread"
    )(half)
    rows, operand = call(order_kernel, "order", [arr(tall, 2 * n), arr(2 * n, 4 * dims, dtype=BF16)], 3)(place, *sides)
    corners = [[p * 4 + k for p in range(PLACES)] for k in range(4)]
    near = lax.all_to_all(copies, "cell", 0, 0, axis_index_groups=corners, tiled=True)
    near, rows = lax.optimization_barrier((near, rows))
    rows1 = sent(rows, lambda l, c, z, f, y, h: (1 - l, c, z, f, y, h))
    far = swapped(near)

    bufs = [pltpu.VMEM((2 * n, 2 * n), F32)] * 2
    pair = [pltpu.VMEM((2 * n, LANES), F32)] * 2
    part = call(first_kernel, "first", arr(1, 2 * n), 3, bufs + pair)(place, operand, near)
    part = call(first_kernel, "first_far", arr(1, 2 * n), 4, bufs + pair)(place, operand, far, part)
    parts = [
        sent(part, lambda l, c, z, f, y, h, j=j, k=k: (1 - l, c, z, f, y ^ j, h ^ k)) for j in (0, 1) for k in (0, 1)
    ]
    cols, extra = call(
        split_kernel, "split", [arr(2 * PLACES, 3 * dims, n // 2, dtype=BF16), arr(2 * PLACES, 8, n // 2)], 3
    )(place, near, far)
    belief1, mine = call(
        functools.partial(second_kernel, offset), "second", [arr(1, n), arr(2 * PLACES, lines, LANES)], 7, bufs
    )(place, rows1, cols, *parts)
    sixteen = [
        [device(l, c, z, f, y, h) for c in (0, 1) for z in range(DEPTHS) for f in (0, 1)]
        for l in (0, 1)
        for y in (0, 1)
        for h in (0, 1)
    ]
    seen = lax.all_to_all(mine, ("tm", "cell"), 0, 0, axis_index_groups=sixteen, tiled=True)
    seen, belief1 = lax.optimization_barrier((seen, belief1))
    belief1 = sent(belief1, lambda l, c, z, f, y, h: (1 - l, c ^ y ^ 1, z, f, y, h))
    belief2, part = call(
        functools.partial(third_kernel, offset),
        "third",
        [arr(1, n), arr(1, 2 * n)],
        5,
        bufs + pair + [pltpu.VMEM((lines, LANES), F32), pltpu.VMEM((2 * PLACES, n // 2), F32)],
    )(place, operand, cols, extra, seen)
    part, belief1 = lax.optimization_barrier((part, belief1))
    parts = [
        sent(part, lambda l, c, z, f, y, h, j=j, k=k: (l, c ^ y ^ j ^ 1, z, f, y ^ j, h ^ k))
        for j in (0, 1)
        for k in (0, 1)
    ]
    return call(last_kernel, "last", arr(1, n), 9)(place, potentials, base, belief1, belief2, *parts)


def solution(mesh):
    return jax.shard_map(
        body,
        mesh=mesh,
        in_specs=(P("tm", None, "cell"), P("tm", "cell")),
        out_specs=P("tm", "cell"),
        check_vma=False,
    )
```
